32 devices in a mesh: lon: 8 (over z, y), lat: 4 (over x, core).
Axes of the slice: x: 2, y: 2, z: 4, core: 2. Of those that a mesh axis runs over, the one named last changes fastest.
Arguments:
- height: float32 [1024, 128, 512], P(None, 'lon', 'lat'), may hold values from -1 to 1
- land_sea: int32 [128, 512], P('lon', 'lat'), may hold values 0 or 1
- patterns: bfloat16 [512, 2, 128, 512], P(None, None, 'lon', 'lat'), may hold values from -0.0234375 to 0.0234375
Outputs:
- covariance: float32 [8, 512, 512], P('lon', 'lat')
The draws below stay inside these ranges and needn't reach their ends.
All inputs are finite; a program needn't handle non-finite values. No bound on the sum of `land_sea` on one device may be relied on, other than what follows from the above.
Results may differ from the reference program's by a relative error of at most 0.0003.
The reference program's roundings to bfloat16 on the way count: a program that leaves them out, or rounds other values in their place, can miss the bound.
Values sent between devices are 32-bit elements; how exact they have to be, the bound alone decides.
No kernel may reach another device: no remote copies, remote signals or barrier semaphores. Data moves between devices by JAX's collectives and lax.ppermute only.
A program may use at most 128 MiB of HBM per device.

```python
import math
import jax
import jax.numpy as jnp
from jax import lax

TIMES = 1024
K = 512
NLON = 128
NLAT = 512
LAGS = 8


def draw_height(key, part):
    first, second = jax.random.split(key, 2)
    shape = (TIMES, NLON, NLAT)
    ramp = 1.0 + 2.0 * jnp.arange(NLON, dtype=jnp.float32) / max(NLON - 1, 1)
    rough = jax.random.uniform(second, shape, jnp.float32, 0.5, 1.5)
    noise = jax.random.truncated_normal(first, -4.0, 4.0, shape, jnp.float32)
    return 0.05 * ramp[:, None] * rough * noise


def set_ends(drawn, stream_key, smallest, largest):
    extent = drawn.shape
    index_at = [jax.random.randint(jax.random.fold_in(stream_key, axis), (), 0, extent[axis]) for axis in range(len(extent))]
    drawn = drawn.at[tuple(index_at)].set(smallest)
    longest = extent.index(max(extent))
    index_at[longest] = (index_at[longest] + 1) % extent[longest]
    return drawn.at[tuple(index_at)].set(largest)


def spiked(result, key, source, target, shards_of, factor):
    owner, partner = [(jnp.arange(result.shape[position]) // (result.shape[position] // shards_of)).reshape([-1 if axis == position else 1 for axis in range(result.ndim)]) for position in (source, target)]
    chosen = jax.random.permutation(key, shards_of)[partner]
    strong = (owner == chosen) | (owner == (partner + shards_of // 2) % shards_of)
    return jnp.where(strong, factor * result, result)


def level_of(key, shape, pieces, least, top_value):
    gain, own = 1.0, jax.random.fold_in(key, 6)
    for axis_at, shards_of in pieces:
        heights = jnp.exp(jax.random.uniform(jax.random.fold_in(own, axis_at), (shards_of,), jnp.float32, least / len(pieces), top_value / len(pieces)))
        gain = gain * jnp.repeat(heights, shape[axis_at] // shards_of).reshape([-1 if axis == axis_at else 1 for axis in range(len(shape))])
    return gain


def noise_with(own_key, shape, scale, reach, shards, heavy, held_as=jnp.bfloat16):
    array = scale * jax.random.normal(own_key, shape, jnp.float32)
    if shards:
        array = array * level_of(own_key, shape, shards, -0.22, 0.18)
    return jnp.clip(spiked(array, jax.random.fold_in(own_key, 3), *heavy), -reach, reach).astype(held_as)


def setup_inputs(seed: int = 0) -> dict:
    key_of = jax.random.split(jax.random.key(seed), 4)
    return {
        "height": draw_height(jax.random.fold_in(key_of[3], 71), 0),
        "land_sea": set_ends((jax.random.randint(key_of[1], (NLON, NLAT), 0, 5) < 4).astype(jnp.int32), jax.random.fold_in(key_of[1], 1), 0, 1),
        "patterns": noise_with(key_of[2], (K, 2, NLON, NLAT), (2 * NLON * NLAT) ** -0.5, 0.0234375, ((2, 8), (3, 4)), (2, 0, 8, 2.0)),
    }


GRAVITY = 9.81
ROTATION = 7.2921e-05
EARTH_RADIUS = 6371000.0
LAT_SOUTH = 20.0
LAT_SPAN = 45.0
LON_STEP = 1.0 / 12.0

def stencil_coefs(rows_index, total_rows):
    degrees = LAT_SOUTH + LAT_SPAN * (rows_index.astype(jnp.float32) + 0.5) / total_rows
    radians = degrees * (math.pi / 180.0)
    coriolis = 2.0 * ROTATION * jnp.sin(radians)
    north_step = EARTH_RADIUS * (LAT_SPAN / total_rows) * (math.pi / 180.0)
    east_step = EARTH_RADIUS * jnp.cos(radians) * (LON_STEP * math.pi / 180.0)
    return (-GRAVITY / (coriolis * 2.0 * north_step), GRAVITY / (coriolis * 2.0 * east_step))

def velocities(padded, coef_east, coef_north, ocean):
    lat_diff = padded[:, 1:-1, 2:] - padded[:, 1:-1, :-2]
    lon_diff = padded[:, 2:, 1:-1] - padded[:, :-2, 1:-1]
    return (coef_east * lat_diff * ocean, coef_north * lon_diff * ocean)

def reference(height, land_sea, patterns):
    ocean = land_sea.astype(jnp.float32)
    coef_east, coef_north = stencil_coefs(jnp.arange(NLAT, dtype=jnp.int32), NLAT)
    flat_patterns = patterns.reshape(K, 2 * NLON * NLAT)
    blocks = height.reshape(TIMES // 32, 32, NLON, NLAT)

    def one_block(days):
        padded = jnp.pad(days, ((0, 0), (1, 1), (1, 1)))
        east_vel, north_vel = velocities(padded, coef_east, coef_north, ocean)
        energy = jnp.sum(east_vel * east_vel + north_vel * north_vel)
        stacked = jnp.stack([east_vel, north_vel], axis=1).astype(jnp.bfloat16).reshape(32, 2 * NLON * NLAT)
        part = lax.dot_general(flat_patterns, stacked, (((1,), (1,)), ((), ())), preferred_element_type=jnp.float32)
        return (part, energy)
    parts, energies = lax.map(one_block, blocks)
    totals = jnp.transpose(parts, (1, 0, 2)).reshape(K, TIMES)
    energy = jnp.sum(energies)
    centered = totals - lax.optimization_barrier(jnp.mean(totals, axis=1, keepdims=True))
    normed = centered / jnp.sqrt(energy / (2.0 * TIMES * NLON * NLAT) + 1e-06)
    padded_modes = jnp.concatenate([normed, jnp.zeros_like(normed)], axis=1)

    def one_lag(lag):
        shifted = lax.dynamic_slice_in_dim(padded_modes, lag, TIMES, 1)
        product = lax.dot_general(shifted, normed, (((1,), (1,)), ((), ())), precision=lax.Precision.HIGHEST, preferred_element_type=jnp.float32)
        return product / (TIMES - lag).astype(jnp.float32)
    return lax.map(one_lag, jnp.arange(LAGS, dtype=jnp.int32))
```

```python
import functools
import math

import jax
import jax.numpy as jnp
from jax import lax
from jax.experimental import pallas as pl
from jax.experimental.pallas import tpu as pltpu
from jax.sharding import PartitionSpec as P

GRAVITY = 9.81
ROTATION = 7.2921e-05
EARTH_RADIUS = 6371000.0
LAT_SOUTH = 20.0
LAT_SPAN = 45.0
LON_STEP = 1.0 / 12.0

F32 = jnp.float32
BF16 = jnp.bfloat16
BOTH = ("lon", "lat")
LANES = 128
TILE = 8
DAY_BLOCK = 256
SPLIT = 8
VMEM = pl.BlockSpec(memory_space=pltpu.VMEM)
SMEM = pl.BlockSpec(memory_space=pltpu.SMEM)
ANY = pl.BlockSpec(memory_space=pl.ANY)
NT = (((1,), (1,)), ((), ()))
NN = (((1,), (0,)), ((), ()))


def like(*shape, dtype=F32):
    return jax.ShapeDtypeStruct(shape, dtype)


def params(mib=48):
    return pltpu.CompilerParams(vmem_limit_bytes=mib << 20)


def stencil_coefs(rows_index, total_rows):
    degrees = LAT_SOUTH + LAT_SPAN * (rows_index.astype(F32) + 0.5) / total_rows
    radians = degrees * (math.pi / 180.0)
    coriolis = 2.0 * ROTATION * jnp.sin(radians)
    north_step = EARTH_RADIUS * (LAT_SPAN / total_rows) * (math.pi / 180.0)
    east_step = EARTH_RADIUS * jnp.cos(radians) * (LON_STEP * math.pi / 180.0)
    return (-GRAVITY / (coriolis * 2.0 * north_step), GRAVITY / (coriolis * 2.0 * east_step))


def edge_rows_kernel(chunks, height, *refs):
    outs, sems = refs[:-1], refs[-1]
    last = height.shape[1] - 1
    copies = []
    for at, (start, size) in enumerate(chunks):
        for side, row in enumerate((0, last)):
            copies.append(
                pltpu.make_async_copy(
                    height.at[pl.ds(start, size), row, :], outs[2 * at + side], sems.at[2 * at + side]
                )
            )
    for copy in copies:
        copy.start()
    for copy in copies:
        copy.wait()


def edge_rows(height, chunks):
    lanes = height.shape[2]
    shapes = [like(size, lanes) for _, size in chunks for _ in range(2)]
    return pl.pallas_call(
        functools.partial(edge_rows_kernel, chunks),
        out_shape=shapes,
        in_specs=[ANY],
        out_specs=[VMEM] * len(shapes),
        scratch_shapes=[pltpu.SemaphoreType.DMA((len(shapes),))],
    )(height)


def interior_kernel(
    order, height, coefs, patterns,
    totals, energy, near_rows, edge_cols, row_patterns, col_patterns,
    flat, velocity,
):
    cells, lanes = coefs.shape[1:]
    days = height.shape[0] // cells
    modes = patterns.shape[0]
    north_at = cells * lanes
    block = modes // SPLIT
    group_days = lanes // 4
    size = 16 * cells
    step = pl.program_id(0)
    to, source = (lax.broadcasted_iota(jnp.int32, (size, size), dim) for dim in (0, 1))
    swap = ((to // 16 == source % cells) & (to % 16 == source // cells)).astype(BF16)

    @pl.when(step == 0)
    def _():
        energy[...] = jnp.zeros_like(energy)

        @pl.loop(0, modes // 16, unroll=8)
        def _(group):
            at = group * 16
            source_row = order[at // block] * block + at % block
            both = jnp.concatenate(
                [
                    patterns[pl.ds(source_row, 16), side].reshape(size, lanes)
                    for side in range(2)
                ],
                axis=1,
            )
            moved = lax.dot_general(swap, both, NN, preferred_element_type=F32).astype(BF16)
            here = pl.ds(pl.multiple_of(at, 16), 16)
            for cell in range(cells):
                rows = slice(cell * 16, cell * 16 + 16)
                flat[here, cell * lanes : (cell + 1) * lanes] = moved[rows, :lanes]
                north = moved[rows, lanes:]
                if cell == 0:
                    row_patterns[here, :lanes] = north
                elif cell == cells - 1:
                    row_patterns[here, lanes:] = north
                else:
                    place = north_at + (cell - 1) * lanes
                    flat[here, place : place + lanes] = north

        width = 2 * cells
        place, column = (lax.broadcasted_iota(jnp.int32, (cells * lanes, width), d) for d in (0, 1))
        wanted = (column % cells) * lanes + (column // cells) * (lanes - 1)
        pick = (place == wanted).astype(BF16)
        col_patterns[...] = lax.dot_general(
            flat[:, :north_at], pick, NN, preferred_element_type=F32
        ).astype(BF16)

    lane = lax.broadcasted_iota(jnp.int32, (TILE, lanes), 1)
    row = lax.broadcasted_iota(jnp.int32, (TILE, lanes), 0)
    inner = (lane > 0) & (lane < lanes - 1)
    east_coefs = [jnp.where(inner, coefs[0, at : at + TILE, :], 0.0) for at in (0, TILE)]
    north_coefs = [coefs[1, 1 : 1 + TILE, :], jnp.where(row < 2, 0.0, coefs[1, 7 : 7 + TILE, :])]

    def some_days(group, gathered):
        gathered = list(gathered)
        total = jnp.zeros((TILE, lanes), F32)
        easts, norths = [], []
        for day in range(16):
            base = pl.multiple_of((group * 16 + day) * cells, cells)
            halves = [height[pl.ds(base + at, TILE), :] for at in (0, TILE)]
            inside = [height[pl.ds(base + at, TILE), :] for at in (2, 6)]
            diffs = [inside[0] - halves[0], halves[1] - inside[1]]
            for side in range(2):
                plane = halves[side]
                east = pltpu.roll(plane, lanes - 1, 1) - pltpu.roll(plane, 1, 1)
                east = east * east_coefs[side]
                north = diffs[side] * north_coefs[side]
                total = total + east * east + north * north
                easts.append(east)
                norths.append(north)
                place = (group % 2) * 16 + day
                turn = pltpu.roll(plane, 4 * place + 2, 1)
                gathered[side] = jnp.where(lane // 4 == place, turn, gathered[side])
        both = jnp.concatenate(
            [jnp.concatenate(easts).astype(BF16), jnp.concatenate(norths).astype(BF16)], axis=1
        )
        moved = lax.dot_general(swap, both, NN, preferred_element_type=F32).astype(BF16)
        here = pl.ds(pl.multiple_of(group * 16, 16), 16)
        for cell in range(cells):
            rows = slice(cell * 16, cell * 16 + 16)
            velocity[here, cell * lanes : (cell + 1) * lanes] = moved[rows, :lanes]
            if cell < TILE or cell > TILE + 1:
                place = north_at + (cell if cell < TILE else cell - 2) * lanes
                velocity[here, place : place + lanes] = moved[rows, lanes:]
        return gathered, total

    def two_groups(pair, carry):
        zero = jnp.zeros((TILE, lanes), F32)
        gathered, first = some_days(pair * 2, [zero, zero])
        gathered, second = some_days(pair * 2 + 1, gathered)
        energy[...] += first + second
        here = pl.ds(pl.multiple_of(pair * lanes, lanes), lanes)
        for side in range(2):
            edge_cols[side * TILE : (side + 1) * TILE, here] = gathered[side]
        return carry

    lax.fori_loop(0, days // group_days, two_groups, 0, unroll=4)
    for side, cell in enumerate((1, cells - 2)):
        near_rows[side] = height[pl.ds(cell, days, stride=cells), :]
    totals[...] = lax.dot_general(flat[...], velocity[...], NT, preferred_element_type=F32)


def interior(order, height, coefs, patterns):
    days, cells, lanes = height.shape
    modes = patterns.shape[0]
    depth = (2 * cells - 2) * lanes
    day = min(DAY_BLOCK, days)
    return pl.pallas_call(
        interior_kernel,
        grid=(days // day,),
        out_shape=[
            like(modes, days),
            like(TILE, lanes),
            like(2, days, lanes),
            like(cells, 4 * days),
            like(modes, 2 * lanes, dtype=BF16),
            like(modes, 2 * cells, dtype=BF16),
        ],
        in_specs=[
            SMEM,
            pl.BlockSpec((day * cells, lanes), lambda s: (s, 0)),
            pl.BlockSpec((2, cells, lanes), lambda s: (0, 0, 0)),
            pl.BlockSpec(
                patterns.shape, lambda s: (0, 0, 0, 0), pipeline_mode=pl.Buffered(1)
            ),
        ],
        out_specs=[
            pl.BlockSpec((modes, day), lambda s: (0, s)),
            pl.BlockSpec((TILE, lanes), lambda s: (0, 0)),
            pl.BlockSpec((2, day, lanes), lambda s: (0, s, 0)),
            pl.BlockSpec((cells, 4 * day), lambda s: (0, s)),
            pl.BlockSpec((modes, 2 * lanes), lambda s: (0, 0)),
            pl.BlockSpec((modes, 2 * cells), lambda s: (0, 0)),
        ],
        scratch_shapes=[
            pltpu.VMEM((modes, depth), BF16),
            pltpu.VMEM((day, depth), BF16),
        ],
        compiler_params=params(),
        cost_estimate=pl.CostEstimate(
            flops=2 * modes * depth * days, bytes_accessed=14 << 20, transcendentals=0
        ),
    )(order, height.reshape(days * cells, lanes), coefs, patterns)


def edge_kernel(
    with_energy, totals, before, after, near_rows, west, east, edge_cols, coefs, row_patterns,
    col_patterns, energy, keep, send,
):
    cells, lanes = coefs.shape[1:]
    days = totals.shape[1]
    low = (near_rows[0] - before[...]) * coefs[1, 0:1, :]
    high = (after[...] - near_rows[1]) * coefs[1, cells - 1 : cells, :]
    rows = jnp.concatenate([low.astype(BF16), high.astype(BF16)], axis=1)
    added = lax.dot_general(row_patterns[...], rows, NT, preferred_element_type=F32)
    four = lax.broadcasted_iota(jnp.int32, (cells, 4 * days), 1) % 4
    left = (edge_cols[...] - pltpu.roll(west[...], 2, 1)) * coefs[0, :, 0:1]
    right = (east[...] - pltpu.roll(edge_cols[...], 2, 1)) * coefs[0, :, lanes - 1 : lanes]
    both = jnp.where(four == 3, left, jnp.where(four == 2, right, 0.0))
    packed = both.astype(BF16)
    wide = 4 * lanes
    packed = jnp.concatenate([packed[:, at : at + wide] for at in range(0, 4 * days, wide)], axis=0)
    place, column = (lax.broadcasted_iota(jnp.int32, (wide, 2 * lanes), d) for d in (0, 1))
    pick = (place == 4 * (column % lanes) + 3 - column // lanes).astype(BF16)
    sides = lax.dot_general(packed, pick, NN, preferred_element_type=F32).astype(BF16)
    cols = jnp.concatenate(
        [
            jnp.concatenate([sides[at : at + cells, :lanes], sides[at : at + cells, lanes:]], axis=0)
            for at in range(0, sides.shape[0], cells)
        ],
        axis=1,
    )
    added = added + lax.dot_general(col_patterns[...], cols, NN, preferred_element_type=F32)
    summed = totals[...] + added
    half = keep.shape[0]
    keep[...] = summed[:half]
    send[:half, :] = summed[half:]
    squares = (low * low + high * high).reshape(-1, TILE, lanes).sum(axis=0)
    across = both * both
    for at in range(0, 4 * days, lanes):
        squares = squares + across[:, at : at + lanes].reshape(-1, TILE, lanes).sum(axis=0)
    send[half:, :] = jnp.zeros((TILE, send.shape[1]), F32)
    if with_energy:
        squares = squares + energy[...]
    send[half:, :lanes] = squares


def edge(chunk, with_energy, totals, before, after, near_rows, west, east, edge_cols, coefs,
         row_patterns, col_patterns, energy):
    start, size = chunk
    at = start // size
    modes = totals.shape[0]
    cells, lanes = coefs.shape[1:]
    half = modes // 2
    whole = lambda a: pl.BlockSpec(a.shape, lambda s: (0,) * a.ndim)
    cols = pl.BlockSpec((cells, 4 * size), lambda s: (0, at))
    return pl.pallas_call(
        functools.partial(edge_kernel, with_energy),
        grid=(1,),
        out_shape=[like(half, size), like(half + TILE, size)],
        in_specs=[
            pl.BlockSpec((modes, size), lambda s: (0, at)),
            whole(before),
            whole(after),
            pl.BlockSpec((2, size, lanes), lambda s: (0, at, 0)),
            cols,
            cols,
            cols,
            whole(coefs),
            whole(row_patterns),
            whole(col_patterns),
            whole(energy),
        ],
        out_specs=[
            pl.BlockSpec((half, size), lambda s: (0, 0)),
            pl.BlockSpec((half + TILE, size), lambda s: (0, 0)),
        ],
        compiler_params=params(),
    )(totals, before, after, near_rows, west, east, edge_cols, coefs, row_patterns, col_patterns,
      energy)


def covariance_kernel(cells_total, chunks, place, order, energy, *refs):
    parts, (out, full, high, low) = refs[:-4], refs[-4:]
    modes, days = full.shape
    block = modes // SPLIT
    per_chunk = len(parts) // len(chunks)
    for at, (start, size) in enumerate(chunks):
        position = 0
        for part in parts[at * per_chunk : (at + 1) * per_chunk]:
            for piece in range(part.shape[0] // block):
                to = pl.ds(pl.multiple_of(order[position] * block, block), block)
                full[to, start : start + size] = part[piece * block : (piece + 1) * block, :]
                position += 1
    centered = full[...] - jnp.sum(full[...], axis=1, keepdims=True) * (1.0 / days)
    full[...] = centered
    upper = centered.astype(BF16)
    high[...] = upper
    low[...] = (centered - upper.astype(F32)).astype(BF16)
    rows = out.shape[1]
    lag = place[1]
    mine = full[pl.ds(pl.multiple_of(place[0] * rows, rows), rows), :]
    mine = pltpu.roll(mine, days - lag, 1)
    day = lax.broadcasted_iota(jnp.int32, mine.shape, 1)
    mine = jnp.where(day < days - lag, mine, 0.0)
    mine_high = mine.astype(BF16)
    mine_low = (mine - mine_high.astype(F32)).astype(BF16)
    dot = lambda a, b: lax.dot_general(a, b, NT, preferred_element_type=F32)
    product = dot(mine_low, high[...]) + dot(mine_high, low[...]) + dot(mine_high, high[...])
    total = jnp.sum(energy[...], axis=(0, 1), keepdims=True)
    spread = total / cells_total + 1e-06
    out[0] = product / (spread * (days - lag).astype(F32))


def covariance(cells_total, chunks, rows, place, order, energy, parts):
    modes = SPLIT * parts[0].shape[0] // 2
    days = sum(size for _, size in chunks)
    return pl.pallas_call(
        functools.partial(covariance_kernel, cells_total, chunks),
        out_shape=like(1, rows, modes),
        in_specs=[SMEM, SMEM] + [VMEM] * (1 + len(parts)),
        out_specs=VMEM,
        scratch_shapes=[
            pltpu.VMEM((modes, days), F32),
            pltpu.VMEM((modes, days), BF16),
            pltpu.VMEM((modes, days), BF16),
        ],
        compiler_params=params(),
    )(place, order, energy, *parts)


def steps_of(devices):
    flips = [(1, 1), (2, 4), (4, 2)] + [(b, b) for b in (8 << i for i in range(30)) if b < devices]
    return [[(i, i ^ flip[i & 1]) for i in range(devices)] for flip in flips]


def block_order(index):
    core, first, second = index & 1, (index >> 1) & 1, (index >> 2) & 1
    order = []
    for position in range(SPLIT):
        near, here, there = position >> 2, (position >> 1) & 1, position & 1
        owner = core ^ near
        a = jnp.where(owner == 0, first ^ here, first ^ there)
        b = jnp.where(owner == 0, second ^ there, second ^ here)
        order.append(owner * 4 + a * 2 + b)
    return jnp.stack(order).astype(jnp.int32)


def reduced(keep, send, steps):
    half = keep.shape[0]
    extra = send[half:]
    for step in range(3):
        got = lax.ppermute(send, BOTH, steps[step])
        half = keep.shape[0]
        quarter = half // 2 if step < 2 else 0
        extra = extra + got[half:]
        send = jnp.concatenate([keep[quarter:] + got[quarter:half], extra], axis=0)
        keep = keep[:quarter] + got[:quarter]
    for step in steps[3:]:
        send = send + lax.ppermute(send, BOTH, step)
    return send


def gathered(own, steps):
    pair = jnp.concatenate([own, lax.ppermute(own, BOTH, steps[2])], axis=0)
    other = lax.ppermute(pair, BOTH, steps[1])
    return [pair, other, lax.ppermute(pair, BOTH, steps[0]), lax.ppermute(other, BOTH, steps[0])]


def on_device(height, land_sea, patterns):
    days, lon_cells, lat_cells = height.shape
    lat_devices = lax.axis_size("lat")
    lon_devices = lax.axis_size("lon")
    total_rows = lat_cells * lat_devices
    lat_place = lax.axis_index("lat")
    lon_place = lax.axis_index("lon")
    mode_count = patterns.shape[0]
    chunks = [(0, days)]
    steps = steps_of(lat_devices * lon_devices)
    up = [(i, i + 1) for i in range(lon_devices - 1)]
    down = [(j, i) for i, j in up]
    right = [(i, i + 1) for i in range(lat_devices - 1)]
    left = [(j, i) for i, j in right]

    edges = edge_rows(height, chunks)
    before = [lax.ppermute(edges[2 * i + 1], "lon", up) for i in range(len(chunks))]
    after = [lax.ppermute(edges[2 * i], "lon", down) for i in range(len(chunks))]

    rows_index = lat_place * lat_cells + jnp.arange(lat_cells, dtype=jnp.int32)
    coef_east, coef_north = stencil_coefs(rows_index, total_rows)
    ocean = land_sea.astype(F32)
    coefs = jnp.stack([coef_east * ocean, coef_north * ocean])
    order = block_order(lon_place * lat_devices + lat_place)
    totals, energy, near_rows, edge_cols, row_patterns, col_patterns = interior(
        order, height, coefs, patterns
    )
    west = lax.ppermute(edge_cols, "lat", right)
    east = lax.ppermute(edge_cols, "lat", left)

    parts = []
    for i, chunk in enumerate(chunks):
        last = i == len(chunks) - 1
        keep, send = edge(
            chunk, last, totals, before[i], after[i], near_rows, west, east, edge_cols, coefs,
            row_patterns, col_patterns, energy,
        )
        own = reduced(keep, send, steps)
        block = mode_count // SPLIT
        if last:
            energy = own[block:, :LANES]
            own = own[:block]
        parts.extend(gathered(own, steps))
    cells_total = 2.0 * days * lon_cells * lon_devices * total_rows
    place = jnp.stack([lat_place, lon_place]).astype(jnp.int32)
    return covariance(
        cells_total, chunks, mode_count // lat_devices, place, order, energy, parts
    )


def solution(mesh):
    placed = (P(None, "lon", "lat"), P("lon", "lat"), P(None, None, "lon", "lat"))
    return jax.shard_map(
        on_device, mesh=mesh, in_specs=placed, out_specs=P("lon", "lat", None), check_vma=False
    )
```

```python
import functools
import math

import jax
import jax.numpy as jnp
from jax import lax
from jax.experimental import pallas as pl
from jax.experimental.pallas import tpu as pltpu
from jax.sharding import PartitionSpec as P

GRAVITY = 9.81
ROTATION = 7.2921e-05
EARTH_RADIUS = 6371000.0
LAT_SOUTH = 20.0
LAT_SPAN = 45.0
LON_STEP = 1.0 / 12.0

F32 = jnp.float32
BF16 = jnp.bfloat16
BOTH = ("lon", "lat")
LANES = 128
TILE = 8
DAY_BLOCK = 256
SCATTERS = 4
SPLIT = 2**SCATTERS
VMEM = pl.BlockSpec(memory_space=pltpu.VMEM)
SMEM = pl.BlockSpec(memory_space=pltpu.SMEM)
ANY = pl.BlockSpec(memory_space=pl.ANY)
NT = (((1,), (1,)), ((), ()))
NN = (((1,), (0,)), ((), ()))


def like(*shape, dtype=F32):
    return jax.ShapeDtypeStruct(shape, dtype)


def params(mib=24):
    return pltpu.CompilerParams(vmem_limit_bytes=mib << 20)


def stencil_coefs(rows_index, total_rows):
    degrees = LAT_SOUTH + LAT_SPAN * (rows_index.astype(F32) + 0.5) / total_rows
    radians = degrees * (math.pi / 180.0)
    coriolis = 2.0 * ROTATION * jnp.sin(radians)
    north_step = EARTH_RADIUS * (LAT_SPAN / total_rows) * (math.pi / 180.0)
    east_step = EARTH_RADIUS * jnp.cos(radians) * (LON_STEP * math.pi / 180.0)
    return (-GRAVITY / (coriolis * 2.0 * north_step), GRAVITY / (coriolis * 2.0 * east_step))


def edge_rows_kernel(height, first, last, sems):
    copies = [
        pltpu.make_async_copy(height.at[:, row, :], to, sems.at[at])
        for at, (row, to) in enumerate(((0, first), (height.shape[1] - 1, last)))
    ]
    for copy in copies:
        copy.start()
    for copy in copies:
        copy.wait()


def edge_rows(height):
    days, _, lanes = height.shape
    return pl.pallas_call(
        edge_rows_kernel,
        out_shape=[like(days, lanes)] * 2,
        in_specs=[ANY],
        out_specs=[VMEM] * 2,
        scratch_shapes=[pltpu.SemaphoreType.DMA((2,))],
    )(height)


def interior_kernel(chunks, order, height, coefs, patterns_hbm, *refs):
    totals, refs = refs[: len(chunks)], refs[len(chunks) :]
    energy, near_rows, edge_cols, row_patterns, col_patterns, *refs = refs
    patterns, flat, first, second, sem = refs
    cells, lanes = coefs.shape[1:]
    days = height.shape[0] // cells
    modes = patterns.shape[0]
    north_at = cells * lanes
    block = modes // SPLIT
    group_days = lanes // 4
    size = 16 * cells
    step = pl.program_id(0)
    to, source = (lax.broadcasted_iota(jnp.int32, (size, size), dim) for dim in (0, 1))
    swap = ((to // 16 == source % cells) & (to % 16 == source // cells)).astype(BF16)

    copy = pltpu.make_async_copy(patterns_hbm, patterns, sem)

    def lay_out_patterns():
        @pl.loop(0, modes // 16, unroll=8)
        def _(group):
            at = group * 16
            source_row = order[at // block] * block + at % block
            both = jnp.concatenate(
                [
                    patterns[pl.ds(source_row, 16), side].reshape(size, lanes)
                    for side in range(2)
                ],
                axis=1,
            )
            moved = lax.dot_general(swap, both, NN, preferred_element_type=F32).astype(BF16)
            here = pl.ds(pl.multiple_of(at, 16), 16)
            for cell in range(cells):
                rows = slice(cell * 16, cell * 16 + 16)
                flat[here, cell * lanes : (cell + 1) * lanes] = moved[rows, :lanes]
                north = moved[rows, lanes:]
                if cell == 0:
                    row_patterns[here, :lanes] = north
                elif cell == cells - 1:
                    row_patterns[here, lanes:] = north
                else:
                    place = north_at + (cell - 1) * lanes
                    flat[here, place : place + lanes] = north

        width = 2 * cells
        place, column = (lax.broadcasted_iota(jnp.int32, (cells * lanes, width), d) for d in (0, 1))
        wanted = (column % cells) * lanes + (column // cells) * (lanes - 1)
        pick = (place == wanted).astype(BF16)
        col_patterns[...] = lax.dot_general(
            flat[:, :north_at], pick, NN, preferred_element_type=F32
        ).astype(BF16)

    lane = lax.broadcasted_iota(jnp.int32, (TILE, lanes), 1)
    row = lax.broadcasted_iota(jnp.int32, (TILE, lanes), 0)
    inner = (lane > 0) & (lane < lanes - 1)
    east_coefs = [jnp.where(inner, coefs[0, at : at + TILE, :], 0.0) for at in (0, TILE)]
    north_coefs = [coefs[1, 1 : 1 + TILE, :], jnp.where(row < 2, 0.0, coefs[1, 7 : 7 + TILE, :])]

    def some_days(velocity, group, gathered):
        gathered = list(gathered)
        total = jnp.zeros((TILE, lanes), F32)
        easts, norths = [], []
        for day in range(16):
            base = pl.multiple_of((group * 16 + day) * cells, cells)
            halves = [height[pl.ds(base + at, TILE), :] for at in (0, TILE)]
            inside = [height[pl.ds(base + at, TILE), :] for at in (2, 6)]
            diffs = [inside[0] - halves[0], halves[1] - inside[1]]
            for side in range(2):
                plane = halves[side]
                east = pltpu.roll(plane, lanes - 1, 1) - pltpu.roll(plane, 1, 1)
                east = east * east_coefs[side]
                north = diffs[side] * north_coefs[side]
                total = total + east * east + north * north
                easts.append(east)
                norths.append(north)
                place = (group % 2) * 16 + day
                turn = pltpu.roll(plane, 4 * place + 2, 1)
                gathered[side] = jnp.where(lane // 4 == place, turn, gathered[side])
        both = jnp.concatenate(
            [jnp.concatenate(easts).astype(BF16), jnp.concatenate(norths).astype(BF16)], axis=1
        )
        moved = lax.dot_general(swap, both, NN, preferred_element_type=F32).astype(BF16)
        here = pl.ds(pl.multiple_of(group * 16, 16), 16)
        for cell in range(cells):
            rows = slice(cell * 16, cell * 16 + 16)
            velocity[here, cell * lanes : (cell + 1) * lanes] = moved[rows, :lanes]
            if cell < TILE or cell > TILE + 1:
                place = north_at + (cell if cell < TILE else cell - 2) * lanes
                velocity[here, place : place + lanes] = moved[rows, lanes:]
        return gathered, total

    def two_groups(velocity, pair, carry):
        zero = jnp.zeros((TILE, lanes), F32)
        gathered, one = some_days(velocity, pair * 2, [zero, zero])
        gathered, two = some_days(velocity, pair * 2 + 1, gathered)
        energy[...] += one + two
        here = pl.ds(pl.multiple_of(pair * lanes, lanes), lanes)
        for side in range(2):
            edge_cols[side * TILE : (side + 1) * TILE, here] = gathered[side]
        return carry

    def work_out(velocity):
        lax.fori_loop(
            0, days // group_days, functools.partial(two_groups, velocity), 0, unroll=True
        )
        for side, cell in enumerate((1, cells - 2)):
            near_rows[side] = height[pl.ds(cell, days, stride=cells), :]

    def project(velocity, to):
        to[...] = lax.dot_general(flat[...], velocity[...], NT, preferred_element_type=F32)

    blocks = (chunks[-1][0] + chunks[-1][1]) // days
    for at in range(blocks + 1):

        @pl.when(step == at)
        def _(at=at):
            now, ago = (first, second) if at % 2 == 0 else (second, first)
            if at == 0:
                copy.start()
                energy[...] = jnp.zeros_like(energy)
            else:
                day = (at - 1) * days
                chunk = max(i for i, (start, _) in enumerate(chunks) if start <= day)
                project(ago, totals[chunk])
            if at < blocks:
                work_out(now)
            if at == 0:
                copy.wait()
                lay_out_patterns()


def interior(chunks, order, height, coefs, patterns):
    days, cells, lanes = height.shape
    modes = patterns.shape[0]
    depth = (2 * cells - 2) * lanes
    day = min(DAY_BLOCK, days)
    blocks = days // day
    now = lambda s: jnp.minimum(s, blocks - 1)

    def totals_spec(start, size):
        index = lambda s: (0, jnp.clip(s - 1 - start // day, 0, size // day - 1))
        return pl.BlockSpec((modes, day), index)

    return pl.pallas_call(
        functools.partial(interior_kernel, chunks),
        grid=(blocks + 1,),
        out_shape=[like(modes, size) for _, size in chunks]
        + [
            like(TILE, lanes),
            like(2, days, lanes),
            like(cells, 4 * days),
            like(modes, 2 * lanes, dtype=BF16),
            like(modes, 2 * cells, dtype=BF16),
        ],
        in_specs=[
            SMEM,
            pl.BlockSpec((day * cells, lanes), lambda s: (now(s), 0)),
            pl.BlockSpec((2, cells, lanes), lambda s: (0, 0, 0)),
            ANY,
        ],
        out_specs=[totals_spec(*chunk) for chunk in chunks]
        + [
            pl.BlockSpec((TILE, lanes), lambda s: (0, 0)),
            pl.BlockSpec((2, day, lanes), lambda s: (0, now(s), 0)),
            pl.BlockSpec((cells, 4 * day), lambda s: (0, now(s))),
            pl.BlockSpec((modes, 2 * lanes), lambda s: (0, 0)),
            pl.BlockSpec((modes, 2 * cells), lambda s: (0, 0)),
        ],
        scratch_shapes=[
            pltpu.VMEM(patterns.shape, BF16),
            pltpu.VMEM((modes, depth), BF16),
            pltpu.VMEM((day, depth), BF16),
            pltpu.VMEM((day, depth), BF16),
            pltpu.SemaphoreType.DMA,
        ],
        compiler_params=params(48),
        cost_estimate=pl.CostEstimate(
            flops=2 * modes * depth * days, bytes_accessed=14 << 20, transcendentals=0
        ),
    )(order, height.reshape(days * cells, lanes), coefs, patterns)


def edge_kernel(
    last, place, totals, before, after, near_rows, paired, other, edge_cols, coefs, row_patterns,
    col_patterns, energy, keep, send, *more,
):
    cells, lanes = coefs.shape[1:]
    days = totals.shape[1]
    low = (near_rows[0] - before[...]) * coefs[1, 0:1, :]
    high = (after[...] - near_rows[1]) * coefs[1, cells - 1 : cells, :]
    rows = jnp.concatenate([low.astype(BF16), high.astype(BF16)], axis=1)
    added = lax.dot_general(row_patterns[...], rows, NT, preferred_element_type=F32)
    four = lax.broadcasted_iota(jnp.int32, (cells, 4 * days), 1) % 4
    even = place[0] % 2 == 0
    west = jnp.where(even, other[...], paired[...])
    east = jnp.where(even, paired[...], other[...])
    left = (edge_cols[...] - pltpu.roll(west, 2, 1)) * coefs[0, :, 0:1]
    right = (east - pltpu.roll(edge_cols[...], 2, 1)) * coefs[0, :, lanes - 1 : lanes]
    both = jnp.where(four == 3, left, jnp.where(four == 2, right, 0.0))
    packed = both.astype(BF16)
    wide = 4 * lanes
    packed = jnp.concatenate([packed[:, at : at + wide] for at in range(0, 4 * days, wide)], axis=0)
    place, column = (lax.broadcasted_iota(jnp.int32, (wide, 2 * lanes), d) for d in (0, 1))
    pick = (place == 4 * (column % lanes) + 3 - column // lanes).astype(BF16)
    sides = lax.dot_general(packed, pick, NN, preferred_element_type=F32).astype(BF16)
    cols = jnp.concatenate(
        [
            jnp.concatenate([sides[at : at + cells, :lanes], sides[at : at + cells, lanes:]], axis=0)
            for at in range(0, sides.shape[0], cells)
        ],
        axis=1,
    )
    added = added + lax.dot_general(col_patterns[...], cols, NN, preferred_element_type=F32)
    summed = totals[...] + added
    half = keep.shape[0]
    keep[...] = summed[:half]
    send[:half, :] = summed[half:]
    squares = energy[...] + (low * low + high * high).reshape(-1, TILE, lanes).sum(axis=0)
    across = both * both
    for at in range(0, 4 * days, lanes):
        squares = squares + across[:, at : at + lanes].reshape(-1, TILE, lanes).sum(axis=0)
    if last:
        send[half:, :] = jnp.zeros((TILE, send.shape[1]), F32)
        send[half:, :lanes] = squares
    else:
        more[0][...] = squares


def edge(chunk, last, place, totals, before, after, near_rows, paired, other, edge_cols, coefs,
         row_patterns, col_patterns, energy):
    start, size = chunk
    at = start // size
    modes = totals.shape[0]
    cells, lanes = coefs.shape[1:]
    half = modes // 2
    whole = lambda a: pl.BlockSpec(a.shape, lambda s: (0,) * a.ndim)
    cols = pl.BlockSpec((cells, 4 * size), lambda s: (0, at))
    outs = [like(half, size), like(half + TILE * last, size)]
    if not last:
        outs.append(like(TILE, lanes))
    return pl.pallas_call(
        functools.partial(edge_kernel, last),
        grid=(1,),
        out_shape=outs,
        in_specs=[
            SMEM,
            whole(totals),
            pl.BlockSpec((size, lanes), lambda s: (at, 0)),
            pl.BlockSpec((size, lanes), lambda s: (at, 0)),
            pl.BlockSpec((2, size, lanes), lambda s: (0, at, 0)),
            cols,
            cols,
            cols,
            whole(coefs),
            whole(row_patterns),
            whole(col_patterns),
            whole(energy),
        ],
        out_specs=[whole(a) for a in outs],
        compiler_params=params(),
    )(place, totals, before, after, near_rows, paired, other, edge_cols, coefs, row_patterns,
      col_patterns, energy)


def covariance_kernel(cells_total, chunks, place, order, energy, *refs):
    parts, (out, full, high, low) = refs[:-4], refs[-4:]
    modes, days = full.shape
    block = modes // SPLIT
    per_chunk = len(parts) // len(chunks)
    for at, (start, size) in enumerate(chunks):
        position = 0
        for part in parts[at * per_chunk : (at + 1) * per_chunk]:
            for piece in range(part.shape[0] // block):
                to = pl.ds(pl.multiple_of(order[position] * block, block), block)
                full[to, start : start + size] = part[piece * block : (piece + 1) * block, :]
                position += 1
    centered = full[...] - jnp.sum(full[...], axis=1, keepdims=True) * (1.0 / days)
    full[...] = centered
    upper = centered.astype(BF16)
    high[...] = upper
    low[...] = (centered - upper.astype(F32)).astype(BF16)
    rows = out.shape[1]
    lag = place[1]
    mine = full[pl.ds(pl.multiple_of(place[0] * rows, rows), rows), :]
    mine = pltpu.roll(mine, days - lag, 1)
    day = lax.broadcasted_iota(jnp.int32, mine.shape, 1)
    mine = jnp.where(day < days - lag, mine, 0.0)
    mine_high = mine.astype(BF16)
    mine_low = (mine - mine_high.astype(F32)).astype(BF16)
    dot = lambda a, b: lax.dot_general(a, b, NT, preferred_element_type=F32)
    product = dot(mine_low, high[...]) + dot(mine_high, low[...]) + dot(mine_high, high[...])
    total = jnp.sum(energy[...], axis=(0, 1), keepdims=True)
    spread = total / cells_total + 1e-06
    out[0] = product / (spread * (days - lag).astype(F32))


def covariance(cells_total, chunks, rows, place, order, energy, parts):
    modes = 4 * parts[0].shape[0]
    days = sum(size for _, size in chunks)
    return pl.pallas_call(
        functools.partial(covariance_kernel, cells_total, chunks),
        out_shape=like(1, rows, modes),
        in_specs=[SMEM, SMEM] + [VMEM] * (1 + len(parts)),
        out_specs=VMEM,
        scratch_shapes=[
            pltpu.VMEM((modes, days), F32),
            pltpu.VMEM((modes, days), BF16),
            pltpu.VMEM((modes, days), BF16),
        ],
        compiler_params=params(),
    )(place, order, energy, *parts)


def steps_of(devices):
    flips = [(1, 1), (2, 4), (4, 2)] + [(b, b) for b in (8 << i for i in range(30)) if b < devices]
    return [[(i, i ^ flip[i & 1]) for i in range(devices)] for flip in flips]


def block_order(index):
    core, first, second, third = (index >> bit & 1 for bit in range(SCATTERS))
    order = []
    for position in range(SPLIT):
        near, here, there, far = (position >> bit & 1 for bit in reversed(range(SCATTERS)))
        owner = core ^ near
        a = jnp.where(owner == 0, first ^ here, first ^ there)
        b = jnp.where(owner == 0, second ^ there, second ^ here)
        order.append(owner * 8 + a * 4 + b * 2 + (third ^ far))
    return jnp.stack(order).astype(jnp.int32)


def reduced(keep, send, steps):
    for step in range(SCATTERS):
        got = lax.ppermute(send, BOTH, steps[step])
        half = keep.shape[0]
        quarter = half // 2 if step < SCATTERS - 1 else 0
        parts = [keep[quarter:] + got[quarter:half]]
        if got.shape[0] > half:
            parts.append(send[-TILE:] + got[half:])
        send = jnp.concatenate(parts, axis=0)
        keep = keep[:quarter] + got[:quarter]
    for step in steps[SCATTERS:]:
        send = send + lax.ppermute(send, BOTH, step)
    return send


def gathered(own, steps):
    pair = jnp.concatenate([own, lax.ppermute(own, BOTH, steps[3])], axis=0)
    four = jnp.concatenate([pair, lax.ppermute(pair, BOTH, steps[2])], axis=0)
    other = lax.ppermute(four, BOTH, steps[1])
    return [four, other, lax.ppermute(four, BOTH, steps[0]), lax.ppermute(other, BOTH, steps[0])]


def on_device(height, land_sea, patterns):
    days, lon_cells, lat_cells = height.shape
    lat_devices = lax.axis_size("lat")
    lon_devices = lax.axis_size("lon")
    total_rows = lat_cells * lat_devices
    lat_place = lax.axis_index("lat")
    lon_place = lax.axis_index("lon")
    mode_count = patterns.shape[0]
    chunks = [(0, days // 2), (days // 2, days // 2)]
    steps = steps_of(lat_devices * lon_devices)
    up = [(i, i + 1) for i in range(lon_devices - 1)]
    down = [(j, i) for i, j in up]

    first, last = edge_rows(height)
    before = lax.ppermute(last, "lon", up)
    after = lax.ppermute(first, "lon", down)

    rows_index = lat_place * lat_cells + jnp.arange(lat_cells, dtype=jnp.int32)
    coef_east, coef_north = stencil_coefs(rows_index, total_rows)
    ocean = land_sea.astype(F32)
    coefs = jnp.stack([coef_east * ocean, coef_north * ocean])
    place = jnp.stack([lat_place, lon_place]).astype(jnp.int32)
    order = block_order(lon_place * lat_devices + lat_place)
    *totals, energy, near_rows, edge_cols, row_patterns, col_patterns = interior(
        chunks, order, height, coefs, patterns
    )
    pairs = [[(i, i ^ 1) for i in range(lat_devices)]]
    pairs.append([(i, ((i + 1) ^ 1) - 1) for i in range(1, lat_devices - 1)])
    paired, other = (lax.ppermute(edge_cols, "lat", pair) for pair in pairs)

    parts = []
    for i, chunk in enumerate(chunks):
        last = i == len(chunks) - 1
        keep, send, *more = edge(
            chunk, last, place, totals[i], before, after, near_rows, paired, other, edge_cols,
            coefs, row_patterns, col_patterns, energy,
        )
        own = reduced(keep, send, steps)
        if last:
            block = mode_count // SPLIT
            own, energy = own[:block], own[block:, :LANES]
        else:
            energy = more[0]
        parts.extend(gathered(own, steps))
    cells_total = 2.0 * days * lon_cells * lon_devices * total_rows
    return covariance(
        cells_total, chunks, mode_count // lat_devices, place, order, energy, parts
    )


def solution(mesh):
    placed = (P(None, "lon", "lat"), P("lon", "lat"), P(None, None, "lon", "lat"))
    return jax.shard_map(
        on_device, mesh=mesh, in_specs=placed, out_specs=P("lon", "lat", None), check_vma=False
    )
```

```python
import functools
import math

import jax
import jax.numpy as jnp
from jax import lax
from jax.experimental import pallas as pl
from jax.experimental.pallas import tpu as pltpu
from jax.sharding import PartitionSpec as P

GRAVITY = 9.81
ROTATION = 7.2921e-05
EARTH_RADIUS = 6371000.0
LAT_SOUTH = 20.0
LAT_SPAN = 45.0
LON_STEP = 1.0 / 12.0

F32 = jnp.float32
BF16 = jnp.bfloat16
BOTH = ("lon", "lat")
LANES = 128
TILE = 8
DAY_BLOCK = 256
SCATTERS = 4
SPLIT = 2**SCATTERS
VMEM = pl.BlockSpec(memory_space=pltpu.VMEM)
SMEM = pl.BlockSpec(memory_space=pltpu.SMEM)
ANY = pl.BlockSpec(memory_space=pl.ANY)
NT = (((1,), (1,)), ((), ()))
NN = (((1,), (0,)), ((), ()))


def like(*shape, dtype=F32):
    return jax.ShapeDtypeStruct(shape, dtype)


def params(mib=24):
    return pltpu.CompilerParams(vmem_limit_bytes=mib << 20)


def stencil_coefs(rows_index, total_rows):
    degrees = LAT_SOUTH + LAT_SPAN * (rows_index.astype(F32) + 0.5) / total_rows
    radians = degrees * (math.pi / 180.0)
    coriolis = 2.0 * ROTATION * jnp.sin(radians)
    north_step = EARTH_RADIUS * (LAT_SPAN / total_rows) * (math.pi / 180.0)
    east_step = EARTH_RADIUS * jnp.cos(radians) * (LON_STEP * math.pi / 180.0)
    return (-GRAVITY / (coriolis * 2.0 * north_step), GRAVITY / (coriolis * 2.0 * east_step))


def edge_rows_kernel(height, first, last, sems):
    copies = [
        pltpu.make_async_copy(height.at[:, row, :], to, sems.at[at])
        for at, (row, to) in enumerate(((0, first), (height.shape[1] - 1, last)))
    ]
    for copy in copies:
        copy.start()
    for copy in copies:
        copy.wait()


def edge_rows(height):
    days, _, lanes = height.shape
    return pl.pallas_call(
        edge_rows_kernel,
        out_shape=[like(days, lanes)] * 2,
        in_specs=[ANY],
        out_specs=[VMEM] * 2,
        scratch_shapes=[pltpu.SemaphoreType.DMA((2,))],
    )(height)


def interior_kernel(chunks, order, height, coefs, patterns_hbm, *refs):
    totals, refs = refs[: len(chunks)], refs[len(chunks) :]
    energy, near_rows, edge_cols, sent_cols, row_patterns, col_patterns, *refs = refs
    patterns, flat, first, second, sem = refs
    cells, lanes = coefs.shape[1:]
    days = height.shape[0] // cells
    modes = patterns.shape[0]
    north_at = cells * lanes
    block = modes // SPLIT
    group_days = lanes // 4
    size = 16 * cells
    step = pl.program_id(0)
    to, source = (lax.broadcasted_iota(jnp.int32, (size, size), dim) for dim in (0, 1))
    swap = ((to // 16 == source % cells) & (to % 16 == source // cells)).astype(BF16)

    copy = pltpu.make_async_copy(patterns_hbm, patterns, sem)

    def lay_out_patterns():
        @pl.loop(0, modes // 16, unroll=8)
        def _(group):
            at = group * 16
            source_row = order[at // block] * block + at % block
            both = jnp.concatenate(
                [
                    patterns[pl.ds(source_row, 16), side].reshape(size, lanes)
                    for side in range(2)
                ],
                axis=1,
            )
            moved = lax.dot_general(swap, both, NN, preferred_element_type=F32).astype(BF16)
            here = pl.ds(pl.multiple_of(at, 16), 16)
            for cell in range(cells):
                rows = slice(cell * 16, cell * 16 + 16)
                flat[here, cell * lanes : (cell + 1) * lanes] = moved[rows, :lanes]
                north = moved[rows, lanes:]
                if cell == 0:
                    row_patterns[here, :lanes] = north
                elif cell == cells - 1:
                    row_patterns[here, lanes:] = north
                else:
                    place = north_at + (cell - 1) * lanes
                    flat[here, place : place + lanes] = north

        width = 2 * cells
        place, column = (lax.broadcasted_iota(jnp.int32, (cells * lanes, width), d) for d in (0, 1))
        wanted = (column % cells) * lanes + (column // cells) * (lanes - 1)
        pick = (place == wanted).astype(BF16)
        col_patterns[...] = lax.dot_general(
            flat[:, :north_at], pick, NN, preferred_element_type=F32
        ).astype(BF16)

    lane = lax.broadcasted_iota(jnp.int32, (TILE, lanes), 1)
    row = lax.broadcasted_iota(jnp.int32, (TILE, lanes), 0)
    inner = (lane > 0) & (lane < lanes - 1)
    east_coefs = [jnp.where(inner, coefs[0, at : at + TILE, :], 0.0) for at in (0, TILE)]
    north_coefs = [coefs[1, 1 : 1 + TILE, :], jnp.where(row < 2, 0.0, coefs[1, 7 : 7 + TILE, :])]

    def some_days(velocity, group, gathered):
        gathered = list(gathered)
        total = jnp.zeros((TILE, lanes), F32)
        easts, norths = [], []
        for day in range(16):
            base = pl.multiple_of((group * 16 + day) * cells, cells)
            halves = [height[pl.ds(base + at, TILE), :] for at in (0, TILE)]
            inside = [height[pl.ds(base + at, TILE), :] for at in (2, 6)]
            diffs = [inside[0] - halves[0], halves[1] - inside[1]]
            for side in range(2):
                plane = halves[side]
                east = pltpu.roll(plane, lanes - 1, 1) - pltpu.roll(plane, 1, 1)
                east = east * east_coefs[side]
                north = diffs[side] * north_coefs[side]
                total = total + east * east + north * north
                easts.append(east)
                norths.append(north)
                place = (group % 2) * 16 + day
                turn = pltpu.roll(plane, 4 * place + 2, 1)
                gathered[side] = jnp.where(lane // 4 == place, turn, gathered[side])
        both = jnp.concatenate(
            [jnp.concatenate(easts).astype(BF16), jnp.concatenate(norths).astype(BF16)], axis=1
        )
        moved = lax.dot_general(swap, both, NN, preferred_element_type=F32).astype(BF16)
        here = pl.ds(pl.multiple_of(group * 16, 16), 16)
        for cell in range(cells):
            rows = slice(cell * 16, cell * 16 + 16)
            velocity[here, cell * lanes : (cell + 1) * lanes] = moved[rows, :lanes]
            if cell < TILE or cell > TILE + 1:
                place = north_at + (cell if cell < TILE else cell - 2) * lanes
                velocity[here, place : place + lanes] = moved[rows, lanes:]
        return gathered, total

    def two_groups(velocity, pair):
        zero = jnp.zeros((TILE, lanes), F32)
        gathered, one = some_days(velocity, pair * 2, [zero, zero])
        gathered, two = some_days(velocity, pair * 2 + 1, gathered)
        energy[...] += one + two
        edge_cols[:, pair * lanes : (pair + 1) * lanes] = jnp.concatenate(gathered)

    def work_out(velocity):
        pairs = days // group_days
        for pair in range(pairs):
            two_groups(velocity, pair)
        middle = (lane % 4 == 1) | (lane % 4 == 2)
        for pair in range(0, pairs, 2):
            for side in range(0, cells, TILE):
                here = edge_cols[side : side + TILE, pair * lanes : (pair + 1) * lanes]
                there = edge_cols[side : side + TILE, (pair + 1) * lanes : (pair + 2) * lanes]
                both = jnp.where(middle, here, pltpu.roll(there, 2, 1))
                sent_cols[side : side + TILE, pair // 2 * lanes : (pair // 2 + 1) * lanes] = both
        for side, cell in enumerate((1, cells - 2)):
            near_rows[side] = height[pl.ds(cell, days, stride=cells), :]

    def project(velocity, to):
        to[...] = lax.dot_general(flat[...], velocity[...], NT, preferred_element_type=F32)

    blocks = (chunks[-1][0] + chunks[-1][1]) // days
    for at in range(blocks + 1):

        @pl.when(step == at)
        def _(at=at):
            now, ago = (first, second) if at % 2 == 0 else (second, first)
            if at == 0:
                copy.start()
                energy[...] = jnp.zeros_like(energy)
            else:
                day = (at - 1) * days
                chunk = max(i for i, (start, _) in enumerate(chunks) if start <= day)
                project(ago, totals[chunk])
            if at < blocks:
                work_out(now)
            if at == 0:
                copy.wait()
                lay_out_patterns()


def interior(chunks, order, height, coefs, patterns):
    days, cells, lanes = height.shape
    modes = patterns.shape[0]
    depth = (2 * cells - 2) * lanes
    day = min(DAY_BLOCK, days)
    blocks = days // day
    now = lambda s: jnp.minimum(s, blocks - 1)

    def totals_spec(start, size):
        index = lambda s: (0, jnp.clip(s - 1 - start // day, 0, size // day - 1))
        return pl.BlockSpec((modes, day), index)

    return pl.pallas_call(
        functools.partial(interior_kernel, chunks),
        grid=(blocks + 1,),
        out_shape=[like(modes, size) for _, size in chunks]
        + [
            like(TILE, lanes),
            like(2, days, lanes),
            like(cells, 4 * days),
            like(cells, 2 * days),
            like(modes, 2 * lanes, dtype=BF16),
            like(modes, 2 * cells, dtype=BF16),
        ],
        in_specs=[
            SMEM,
            pl.BlockSpec((day * cells, lanes), lambda s: (now(s), 0)),
            pl.BlockSpec((2, cells, lanes), lambda s: (0, 0, 0)),
            ANY,
        ],
        out_specs=[totals_spec(*chunk) for chunk in chunks]
        + [
            pl.BlockSpec((TILE, lanes), lambda s: (0, 0)),
            pl.BlockSpec((2, day, lanes), lambda s: (0, now(s), 0)),
            pl.BlockSpec((cells, 4 * day), lambda s: (0, now(s))),
            pl.BlockSpec((cells, 2 * day), lambda s: (0, now(s))),
            pl.BlockSpec((modes, 2 * lanes), lambda s: (0, 0)),
            pl.BlockSpec((modes, 2 * cells), lambda s: (0, 0)),
        ],
        scratch_shapes=[
            pltpu.VMEM(patterns.shape, BF16),
            pltpu.VMEM((modes, depth), BF16),
            pltpu.VMEM((day, depth), BF16),
            pltpu.VMEM((day, depth), BF16),
            pltpu.SemaphoreType.DMA,
        ],
        compiler_params=params(48),
        cost_estimate=pl.CostEstimate(
            flops=2 * modes * depth * days, bytes_accessed=14 << 20, transcendentals=0
        ),
    )(order, height.reshape(days * cells, lanes), coefs, patterns)


def edge_kernel(
    last, place, totals, before, after, near_rows, paired, other, edge_cols, coefs, row_patterns,
    col_patterns, energy, keep, send, *more,
):
    cells, lanes = coefs.shape[1:]
    days = totals.shape[1]
    low = (near_rows[0] - before[...]) * coefs[1, 0:1, :]
    high = (after[...] - near_rows[1]) * coefs[1, cells - 1 : cells, :]
    rows = jnp.concatenate([low.astype(BF16), high.astype(BF16)], axis=1)
    added = lax.dot_general(row_patterns[...], rows, NT, preferred_element_type=F32)
    four = lax.broadcasted_iota(jnp.int32, (cells, 4 * days), 1) % 4
    even = place[0] % 2 == 0
    spread = []
    for one, two in ((other, paired), (paired, other)):
        halo = jnp.where(even, one[...], two[...])
        blocks = [halo[:, at : at + lanes] for at in range(0, 2 * days, lanes)]
        spread.append([a for b in blocks for a in (b, pltpu.roll(b, lanes - 2, 1))])
    west, east = (jnp.concatenate(a, axis=1) for a in spread)
    left = (edge_cols[...] - pltpu.roll(west, 2, 1)) * coefs[0, :, 0:1]
    right = (east - pltpu.roll(edge_cols[...], 2, 1)) * coefs[0, :, lanes - 1 : lanes]
    both = jnp.where(four == 3, left, jnp.where(four == 2, right, 0.0))
    packed = both.astype(BF16)
    wide = 4 * lanes
    packed = jnp.concatenate([packed[:, at : at + wide] for at in range(0, 4 * days, wide)], axis=0)
    place, column = (lax.broadcasted_iota(jnp.int32, (wide, 2 * lanes), d) for d in (0, 1))
    pick = (place == 4 * (column % lanes) + 3 - column // lanes).astype(BF16)
    sides = lax.dot_general(packed, pick, NN, preferred_element_type=F32).astype(BF16)
    cols = jnp.concatenate(
        [
            jnp.concatenate([sides[at : at + cells, :lanes], sides[at : at + cells, lanes:]], axis=0)
            for at in range(0, sides.shape[0], cells)
        ],
        axis=1,
    )
    added = added + lax.dot_general(col_patterns[...], cols, NN, preferred_element_type=F32)
    summed = totals[...] + added
    half = keep.shape[0]
    keep[...] = summed[:half]
    send[:half, :] = summed[half:]
    squares = energy[...] + (low * low + high * high).reshape(-1, TILE, lanes).sum(axis=0)
    across = both * both
    for at in range(0, 4 * days, lanes):
        squares = squares + across[:, at : at + lanes].reshape(-1, TILE, lanes).sum(axis=0)
    if last:
        send[half:, :] = jnp.zeros((TILE, send.shape[1]), F32)
        send[half:, :lanes] = squares
    else:
        more[0][...] = squares


def edge(chunk, last, place, totals, before, after, near_rows, paired, other, edge_cols, coefs,
         row_patterns, col_patterns, energy):
    start, size = chunk
    at = start // size
    modes = totals.shape[0]
    cells, lanes = coefs.shape[1:]
    half = modes // 2
    whole = lambda a: pl.BlockSpec(a.shape, lambda s: (0,) * a.ndim)
    outs = [like(half, size), like(half + TILE * last, size)]
    if not last:
        outs.append(like(TILE, lanes))
    return pl.pallas_call(
        functools.partial(edge_kernel, last),
        grid=(1,),
        out_shape=outs,
        in_specs=[
            SMEM,
            whole(totals),
            pl.BlockSpec((size, lanes), lambda s: (at, 0)),
            pl.BlockSpec((size, lanes), lambda s: (at, 0)),
            pl.BlockSpec((2, size, lanes), lambda s: (0, at, 0)),
            pl.BlockSpec((cells, 2 * size), lambda s: (0, at)),
            pl.BlockSpec((cells, 2 * size), lambda s: (0, at)),
            pl.BlockSpec((cells, 4 * size), lambda s: (0, at)),
            whole(coefs),
            whole(row_patterns),
            whole(col_patterns),
            whole(energy),
        ],
        out_specs=[whole(a) for a in outs],
        compiler_params=params(),
    )(place, totals, before, after, near_rows, paired, other, edge_cols, coefs, row_patterns,
      col_patterns, energy)


def covariance_kernel(cells_total, chunks, place, order, energy, *refs):
    parts, (out, full, high, low) = refs[:-4], refs[-4:]
    modes, days = full.shape
    block = modes // SPLIT
    per_chunk = len(parts) // len(chunks)
    for at, (start, size) in enumerate(chunks):
        position = 0
        for part in parts[at * per_chunk : (at + 1) * per_chunk]:
            for piece in range(part.shape[0] // block):
                to = pl.ds(pl.multiple_of(order[position] * block, block), block)
                full[to, start : start + size] = part[piece * block : (piece + 1) * block, :]
                position += 1
    centered = full[...] - jnp.sum(full[...], axis=1, keepdims=True) * (1.0 / days)
    full[...] = centered
    upper = centered.astype(BF16)
    high[...] = upper
    low[...] = (centered - upper.astype(F32)).astype(BF16)
    rows = out.shape[1]
    lag = place[1]
    mine = full[pl.ds(pl.multiple_of(place[0] * rows, rows), rows), :]
    mine = pltpu.roll(mine, days - lag, 1)
    day = lax.broadcasted_iota(jnp.int32, mine.shape, 1)
    mine = jnp.where(day < days - lag, mine, 0.0)
    mine_high = mine.astype(BF16)
    mine_low = (mine - mine_high.astype(F32)).astype(BF16)
    dot = lambda a, b: lax.dot_general(a, b, NT, preferred_element_type=F32)
    product = dot(mine_low, high[...]) + dot(mine_high, low[...]) + dot(mine_high, high[...])
    total = jnp.sum(energy[...], axis=(0, 1), keepdims=True)
    spread = total / cells_total + 1e-06
    out[0] = product / (spread * (days - lag).astype(F32))


def covariance(cells_total, chunks, rows, place, order, energy, parts):
    modes = 4 * parts[0].shape[0]
    days = sum(size for _, size in chunks)
    return pl.pallas_call(
        functools.partial(covariance_kernel, cells_total, chunks),
        out_shape=like(1, rows, modes),
        in_specs=[SMEM, SMEM] + [VMEM] * (1 + len(parts)),
        out_specs=VMEM,
        scratch_shapes=[
            pltpu.VMEM((modes, days), F32),
            pltpu.VMEM((modes, days), BF16),
            pltpu.VMEM((modes, days), BF16),
        ],
        compiler_params=params(),
    )(place, order, energy, *parts)


def steps_of(devices):
    flips = [(1, 1), (2, 8), (4, 2), (8, 4)] + [(b, b) for b in (16 << i for i in range(30)) if b < devices]
    return [[(i, i ^ flip[i & 1]) for i in range(devices)] for flip in flips]


def block_order(index):
    core, chip = index & 1, (index >> 1) & 7
    order = []
    for position in range(SPLIT):
        near, here, there, far = (position >> bit & 1 for bit in reversed(range(SCATTERS)))
        owner = core ^ near
        flips = jnp.where(owner == 0, here + there * 2 + far * 4, there + far * 2 + here * 4)
        order.append(owner * 8 + (chip ^ flips))
    return jnp.stack(order).astype(jnp.int32)


def exchanges(keep, send, steps):
    for step in range(SCATTERS):
        got = yield send, steps[step]
        half = keep.shape[0]
        quarter = half // 2 if step < SCATTERS - 1 else 0
        parts = [keep[quarter:] + got[quarter:half]]
        if got.shape[0] > half:
            parts.append(send[half:] + got[half:])
        send = jnp.concatenate(parts, axis=0)
        keep = keep[:quarter] + got[:quarter]
    for step in steps[SCATTERS:]:
        send = send + (yield send, step)
    own, extra = send[:half], send[half:]
    pair = jnp.concatenate([own, (yield own, steps[3])], axis=0)
    four = jnp.concatenate([pair, (yield pair, steps[2])], axis=0)
    other = yield four, steps[1]
    first = yield four, steps[0]
    second = yield other, steps[0]
    return [four, other, first, second], extra


def side_by_side(chains):
    results = [None] * len(chains)
    got = [None] * len(chains)
    while None in results:
        for i, chain in enumerate(chains):
            try:
                send, step = chain.send(got[i])
                got[i] = lax.ppermute(send, BOTH, step)
            except StopIteration as end:
                results[i] = end.value
    return results


def on_device(height, land_sea, patterns):
    days, lon_cells, lat_cells = height.shape
    lat_devices = lax.axis_size("lat")
    lon_devices = lax.axis_size("lon")
    total_rows = lat_cells * lat_devices
    lat_place = lax.axis_index("lat")
    lon_place = lax.axis_index("lon")
    mode_count = patterns.shape[0]
    chunks = [(0, days // 2), (days // 2, days // 2)]
    steps = steps_of(lat_devices * lon_devices)
    up = [(i, i + 1) for i in range(lon_devices - 1)]
    down = [(j, i) for i, j in up]

    first, last = edge_rows(height)
    before = lax.ppermute(last, "lon", up)
    after = lax.ppermute(first, "lon", down)

    rows_index = lat_place * lat_cells + jnp.arange(lat_cells, dtype=jnp.int32)
    coef_east, coef_north = stencil_coefs(rows_index, total_rows)
    ocean = land_sea.astype(F32)
    coefs = jnp.stack([coef_east * ocean, coef_north * ocean])
    place = jnp.stack([lat_place, lon_place]).astype(jnp.int32)
    order = block_order(lon_place * lat_devices + lat_place)
    *totals, energy, near_rows, edge_cols, sent_cols, row_patterns, col_patterns = interior(
        chunks, order, height, coefs, patterns
    )
    pairs = [[(i, i ^ 1) for i in range(lat_devices)]]
    pairs.append([(i, ((i + 1) ^ 1) - 1) for i in range(1, lat_devices - 1)])
    paired, other = (lax.ppermute(sent_cols, "lat", pair) for pair in pairs)

    chains = []
    for i, chunk in enumerate(chunks):
        last = i == len(chunks) - 1
        keep, send, *more = edge(
            chunk, last, place, totals[i], before, after, near_rows, paired, other, edge_cols,
            coefs, row_patterns, col_patterns, energy,
        )
        chains.append(exchanges(keep, send, steps))
        energy = more[0] if more else energy
    results = side_by_side(chains)
    parts = [part for found, _ in results for part in found]
    energy = results[-1][1][:, :LANES]
    cells_total = 2.0 * days * lon_cells * lon_devices * total_rows
    return covariance(
        cells_total, chunks, mode_count // lat_devices, place, order, energy, parts
    )


def solution(mesh):
    placed = (P(None, "lon", "lat"), P("lon", "lat"), P(None, None, "lon", "lat"))
    return jax.shard_map(
        on_device, mesh=mesh, in_specs=placed, out_specs=P("lon", "lat", None), check_vma=False
    )
```

```python
import functools
import math

import jax
import jax.numpy as jnp
from jax import lax
from jax.experimental import pallas as pl
from jax.experimental.pallas import tpu as pltpu
from jax.sharding import PartitionSpec as P

GRAVITY = 9.81
ROTATION = 7.2921e-05
EARTH_RADIUS = 6371000.0
LAT_SOUTH = 20.0
LAT_SPAN = 45.0
LON_STEP = 1.0 / 12.0

F32 = jnp.float32
BF16 = jnp.bfloat16
BOTH = ("lon", "lat")
LANES = 128
TILE = 8
DAY_BLOCK = 256
SCATTERS = 4
SPLIT = 2**SCATTERS
VMEM = pl.BlockSpec(memory_space=pltpu.VMEM)
SMEM = pl.BlockSpec(memory_space=pltpu.SMEM)
ANY = pl.BlockSpec(memory_space=pl.ANY)
NT = (((1,), (1,)), ((), ()))
NN = (((1,), (0,)), ((), ()))


def like(*shape, dtype=F32):
    return jax.ShapeDtypeStruct(shape, dtype)


def params(mib=24):
    return pltpu.CompilerParams(vmem_limit_bytes=mib << 20)


def stencil_coefs(rows_index, total_rows):
    degrees = LAT_SOUTH + LAT_SPAN * (rows_index.astype(F32) + 0.5) / total_rows
    radians = degrees * (math.pi / 180.0)
    coriolis = 2.0 * ROTATION * jnp.sin(radians)
    north_step = EARTH_RADIUS * (LAT_SPAN / total_rows) * (math.pi / 180.0)
    east_step = EARTH_RADIUS * jnp.cos(radians) * (LON_STEP * math.pi / 180.0)
    return (-GRAVITY / (coriolis * 2.0 * north_step), GRAVITY / (coriolis * 2.0 * east_step))


def edge_rows_kernel(height, first, last, sems):
    copies = [
        pltpu.make_async_copy(height.at[:, row, :], to, sems.at[at])
        for at, (row, to) in enumerate(((0, first), (height.shape[1] - 1, last)))
    ]
    for copy in copies:
        copy.start()
    for copy in copies:
        copy.wait()


def edge_rows(height):
    days, _, lanes = height.shape
    return pl.pallas_call(
        edge_rows_kernel,
        out_shape=[like(days, lanes)] * 2,
        in_specs=[ANY],
        out_specs=[VMEM] * 2,
        scratch_shapes=[pltpu.SemaphoreType.DMA((2,))],
    )(height)


def interior_kernel(chunks, order, height, coefs, patterns_hbm, *refs):
    totals, refs = refs[: len(chunks)], refs[len(chunks) :]
    energy, near_rows, edge_cols, sent_cols, row_patterns, col_patterns, *refs = refs
    patterns, flat, first, second, sem = refs
    cells, lanes = coefs.shape[1:]
    days = height.shape[0] // cells
    modes = patterns.shape[0]
    north_at = cells * lanes
    block = modes // SPLIT
    group_days = lanes // 4
    size = 16 * cells
    step = pl.program_id(0)
    to, source = (lax.broadcasted_iota(jnp.int32, (size, size), dim) for dim in (0, 1))
    swap = ((to // 16 == source % cells) & (to % 16 == source // cells)).astype(BF16)

    copy = pltpu.make_async_copy(patterns_hbm, patterns, sem)

    def lay_out_patterns():
        @pl.loop(0, modes // 16, unroll=8)
        def _(group):
            at = group * 16
            source_row = order[at // block] * block + at % block
            both = jnp.concatenate(
                [
                    patterns[pl.ds(source_row, 16), side].reshape(size, lanes)
                    for side in range(2)
                ],
                axis=1,
            )
            moved = lax.dot_general(swap, both, NN, preferred_element_type=F32).astype(BF16)
            here = pl.ds(pl.multiple_of(at, 16), 16)
            for cell in range(cells):
                rows = slice(cell * 16, cell * 16 + 16)
                flat[here, cell * lanes : (cell + 1) * lanes] = moved[rows, :lanes]
                north = moved[rows, lanes:]
                if cell == 0:
                    row_patterns[here, :lanes] = north
                elif cell == cells - 1:
                    row_patterns[here, lanes:] = north
                else:
                    place = north_at + (cell - 1) * lanes
                    flat[here, place : place + lanes] = north

        width = 2 * cells
        place, column = (lax.broadcasted_iota(jnp.int32, (cells * lanes, width), d) for d in (0, 1))
        wanted = (column % cells) * lanes + (column // cells) * (lanes - 1)
        pick = (place == wanted).astype(BF16)
        col_patterns[...] = lax.dot_general(
            flat[:, :north_at], pick, NN, preferred_element_type=F32
        ).astype(BF16)

    lane = lax.broadcasted_iota(jnp.int32, (TILE, lanes), 1)
    row = lax.broadcasted_iota(jnp.int32, (TILE, lanes), 0)
    inner = (lane > 0) & (lane < lanes - 1)
    east_coefs = [jnp.where(inner, coefs[0, at : at + TILE, :], 0.0) for at in (0, TILE)]
    north_coefs = [coefs[1, 1 : 1 + TILE, :], jnp.where(row < 2, 0.0, coefs[1, 7 : 7 + TILE, :])]

    def some_days(velocity, group, gathered):
        gathered = list(gathered)
        total = jnp.zeros((TILE, lanes), F32)
        easts, norths = [], []
        for day in range(16):
            base = pl.multiple_of((group * 16 + day) * cells, cells)
            halves = [height[pl.ds(base + at, TILE), :] for at in (0, TILE)]
            inside = [height[pl.ds(base + at, TILE), :] for at in (2, 6)]
            diffs = [inside[0] - halves[0], halves[1] - inside[1]]
            for side in range(2):
                plane = halves[side]
                east = pltpu.roll(plane, lanes - 1, 1) - pltpu.roll(plane, 1, 1)
                east = east * east_coefs[side]
                north = diffs[side] * north_coefs[side]
                total = total + east * east + north * north
                easts.append(east)
                norths.append(north)
                place = (group % 2) * 16 + day
                turn = pltpu.roll(plane, 4 * place + 2, 1)
                gathered[side] = jnp.where(lane // 4 == place, turn, gathered[side])
        both = jnp.concatenate(
            [jnp.concatenate(easts).astype(BF16), jnp.concatenate(norths).astype(BF16)], axis=1
        )
        moved = lax.dot_general(swap, both, NN, preferred_element_type=F32).astype(BF16)
        here = pl.ds(pl.multiple_of(group * 16, 16), 16)
        for cell in range(cells):
            rows = slice(cell * 16, cell * 16 + 16)
            velocity[here, cell * lanes : (cell + 1) * lanes] = moved[rows, :lanes]
            if cell < TILE or cell > TILE + 1:
                place = north_at + (cell if cell < TILE else cell - 2) * lanes
                velocity[here, place : place + lanes] = moved[rows, lanes:]
        return gathered, total

    def two_groups(velocity, pair):
        zero = jnp.zeros((TILE, lanes), F32)
        gathered, one = some_days(velocity, pair * 2, [zero, zero])
        gathered, two = some_days(velocity, pair * 2 + 1, gathered)
        energy[...] += one + two
        edge_cols[:, pair * lanes : (pair + 1) * lanes] = jnp.concatenate(gathered)

    def work_out(velocity):
        pairs = days // group_days
        for pair in range(pairs):
            two_groups(velocity, pair)
        middle = (lane % 4 == 1) | (lane % 4 == 2)
        for pair in range(0, pairs, 2):
            for side in range(0, cells, TILE):
                here = edge_cols[side : side + TILE, pair * lanes : (pair + 1) * lanes]
                there = edge_cols[side : side + TILE, (pair + 1) * lanes : (pair + 2) * lanes]
                both = jnp.where(middle, here, pltpu.roll(there, 2, 1))
                sent_cols[side : side + TILE, pair // 2 * lanes : (pair // 2 + 1) * lanes] = both
        for side, cell in enumerate((1, cells - 2)):
            near_rows[side] = height[pl.ds(cell, days, stride=cells), :]

    def project(velocity, to):
        to[...] = lax.dot_general(flat[...], velocity[...], NT, preferred_element_type=F32)

    blocks = (chunks[-1][0] + chunks[-1][1]) // days
    for at in range(blocks + 1):

        @pl.when(step == at)
        def _(at=at):
            now, ago = (first, second) if at % 2 == 0 else (second, first)
            if at == 0:
                copy.start()
                energy[...] = jnp.zeros_like(energy)
            else:
                day = (at - 1) * days
                chunk = max(i for i, (start, _) in enumerate(chunks) if start <= day)
                project(ago, totals[chunk])
            if at < blocks:
                work_out(now)
            if at == 0:
                copy.wait()
                lay_out_patterns()


def interior(chunks, order, height, coefs, patterns):
    days, cells, lanes = height.shape
    modes = patterns.shape[0]
    depth = (2 * cells - 2) * lanes
    day = min(DAY_BLOCK, days)
    blocks = days // day
    now = lambda s: jnp.minimum(s, blocks - 1)

    def totals_spec(start, size):
        index = lambda s: (0, jnp.clip(s - 1 - start // day, 0, size // day - 1))
        return pl.BlockSpec((modes, day), index)

    return pl.pallas_call(
        functools.partial(interior_kernel, chunks),
        grid=(blocks + 1,),
        out_shape=[like(modes, size) for _, size in chunks]
        + [
            like(TILE, lanes),
            like(2, days, lanes),
            like(cells, 4 * days),
            like(cells, 2 * days),
            like(modes, 2 * lanes, dtype=BF16),
            like(modes, 2 * cells, dtype=BF16),
        ],
        in_specs=[
            SMEM,
            pl.BlockSpec((day * cells, lanes), lambda s: (now(s), 0)),
            pl.BlockSpec((2, cells, lanes), lambda s: (0, 0, 0)),
            ANY,
        ],
        out_specs=[totals_spec(*chunk) for chunk in chunks]
        + [
            pl.BlockSpec((TILE, lanes), lambda s: (0, 0)),
            pl.BlockSpec((2, day, lanes), lambda s: (0, now(s), 0)),
            pl.BlockSpec((cells, 4 * day), lambda s: (0, now(s))),
            pl.BlockSpec((cells, 2 * day), lambda s: (0, now(s))),
            pl.BlockSpec((modes, 2 * lanes), lambda s: (0, 0)),
            pl.BlockSpec((modes, 2 * cells), lambda s: (0, 0)),
        ],
        scratch_shapes=[
            pltpu.VMEM(patterns.shape, BF16),
            pltpu.VMEM((modes, depth), BF16),
            pltpu.VMEM((day, depth), BF16),
            pltpu.VMEM((day, depth), BF16),
            pltpu.SemaphoreType.DMA,
        ],
        compiler_params=params(48),
        cost_estimate=pl.CostEstimate(
            flops=2 * modes * depth * days, bytes_accessed=14 << 20, transcendentals=0
        ),
    )(order, height.reshape(days * cells, lanes), coefs, patterns)


def edge_kernel(
    last, place, totals, before, after, near_rows, paired, other, edge_cols, coefs, row_patterns,
    col_patterns, energy, keep, send, *more,
):
    cells, lanes = coefs.shape[1:]
    days = totals.shape[1]
    low = (near_rows[0] - before[...]) * coefs[1, 0:1, :]
    high = (after[...] - near_rows[1]) * coefs[1, cells - 1 : cells, :]
    rows = jnp.concatenate([low.astype(BF16), high.astype(BF16)], axis=1)
    added = lax.dot_general(row_patterns[...], rows, NT, preferred_element_type=F32)
    four = lax.broadcasted_iota(jnp.int32, (cells, 4 * days), 1) % 4
    even = place[0] % 2 == 0
    spread = []
    for one, two in ((other, paired), (paired, other)):
        halo = jnp.where(even, one[...], two[...])
        blocks = [halo[:, at : at + lanes] for at in range(0, 2 * days, lanes)]
        spread.append([a for b in blocks for a in (b, pltpu.roll(b, lanes - 2, 1))])
    west, east = (jnp.concatenate(a, axis=1) for a in spread)
    left = (edge_cols[...] - pltpu.roll(west, 2, 1)) * coefs[0, :, 0:1]
    right = (east - pltpu.roll(edge_cols[...], 2, 1)) * coefs[0, :, lanes - 1 : lanes]
    both = jnp.where(four == 3, left, jnp.where(four == 2, right, 0.0))
    packed = both.astype(BF16)
    wide = 4 * lanes
    packed = jnp.concatenate([packed[:, at : at + wide] for at in range(0, 4 * days, wide)], axis=0)
    place, column = (lax.broadcasted_iota(jnp.int32, (wide, 2 * lanes), d) for d in (0, 1))
    pick = (place == 4 * (column % lanes) + 3 - column // lanes).astype(BF16)
    sides = lax.dot_general(packed, pick, NN, preferred_element_type=F32).astype(BF16)
    cols = jnp.concatenate(
        [
            jnp.concatenate([sides[at : at + cells, :lanes], sides[at : at + cells, lanes:]], axis=0)
            for at in range(0, sides.shape[0], cells)
        ],
        axis=1,
    )
    added = added + lax.dot_general(col_patterns[...], cols, NN, preferred_element_type=F32)
    summed = totals[...] + added
    half = keep.shape[0]
    keep[...] = summed[:half]
    send[:half, :] = summed[half:]
    squares = energy[...] + (low * low + high * high).reshape(-1, TILE, lanes).sum(axis=0)
    across = both * both
    for at in range(0, 4 * days, lanes):
        squares = squares + across[:, at : at + lanes].reshape(-1, TILE, lanes).sum(axis=0)
    if last:
        send[half:, :] = jnp.zeros((TILE, send.shape[1]), F32)
        send[half:, :lanes] = squares
    else:
        more[0][...] = squares


def edge(chunk, last, place, totals, before, after, near_rows, paired, other, edge_cols, coefs,
         row_patterns, col_patterns, energy):
    start, size = chunk
    at = start // size
    modes = totals.shape[0]
    cells, lanes = coefs.shape[1:]
    half = modes // 2
    whole = lambda a: pl.BlockSpec(a.shape, lambda s: (0,) * a.ndim)
    outs = [like(half, size), like(half + TILE * last, size)]
    if not last:
        outs.append(like(TILE, lanes))
    return pl.pallas_call(
        functools.partial(edge_kernel, last),
        grid=(1,),
        out_shape=outs,
        in_specs=[
            SMEM,
            whole(totals),
            pl.BlockSpec((size, lanes), lambda s: (at, 0)),
            pl.BlockSpec((size, lanes), lambda s: (at, 0)),
            pl.BlockSpec((2, size, lanes), lambda s: (0, at, 0)),
            pl.BlockSpec((cells, 2 * size), lambda s: (0, at)),
            pl.BlockSpec((cells, 2 * size), lambda s: (0, at)),
            pl.BlockSpec((cells, 4 * size), lambda s: (0, at)),
            whole(coefs),
            whole(row_patterns),
            whole(col_patterns),
            whole(energy),
        ],
        out_specs=[whole(a) for a in outs],
        compiler_params=params(),
    )(place, totals, before, after, near_rows, paired, other, edge_cols, coefs, row_patterns,
      col_patterns, energy)


def covariance_kernel(cells_total, chunks, place, order, energy, *refs):
    parts, (out, full, high, low) = refs[:-4], refs[-4:]
    modes, days = full.shape
    block = modes // SPLIT
    per_chunk = len(parts) // len(chunks)
    for at, (start, size) in enumerate(chunks):
        position = 0
        for part in parts[at * per_chunk : (at + 1) * per_chunk]:
            for piece in range(part.shape[0] // block):
                to = pl.ds(pl.multiple_of(order[position] * block, block), block)
                full[to, start : start + size] = part[piece * block : (piece + 1) * block, :]
                position += 1
    centered = full[...] - jnp.sum(full[...], axis=1, keepdims=True) * (1.0 / days)
    full[...] = centered
    upper = centered.astype(BF16)
    high[...] = upper
    low[...] = (centered - upper.astype(F32)).astype(BF16)
    rows = out.shape[1]
    lag = place[1]
    mine = full[pl.ds(pl.multiple_of(place[0] * rows, rows), rows), :]
    mine = pltpu.roll(mine, days - lag, 1)
    day = lax.broadcasted_iota(jnp.int32, mine.shape, 1)
    mine = jnp.where(day < days - lag, mine, 0.0)
    mine_high = mine.astype(BF16)
    mine_low = (mine - mine_high.astype(F32)).astype(BF16)
    dot = lambda a, b: lax.dot_general(a, b, NT, preferred_element_type=F32)
    both = dot(jnp.concatenate([mine_high, mine_low], axis=0), high[...])
    product = both[rows:] + dot(mine_high, low[...]) + both[:rows]
    total = jnp.sum(energy[...], axis=(0, 1), keepdims=True)
    spread = total / cells_total + 1e-06
    out[0] = product / (spread * (days - lag).astype(F32))


def covariance(cells_total, chunks, rows, place, order, energy, parts):
    modes = 4 * parts[0].shape[0]
    days = sum(size for _, size in chunks)
    return pl.pallas_call(
        functools.partial(covariance_kernel, cells_total, chunks),
        out_shape=like(1, rows, modes),
        in_specs=[SMEM, SMEM] + [VMEM] * (1 + len(parts)),
        out_specs=VMEM,
        scratch_shapes=[
            pltpu.VMEM((modes, days), F32),
            pltpu.VMEM((modes, days), BF16),
            pltpu.VMEM((modes, days), BF16),
        ],
        compiler_params=params(),
    )(place, order, energy, *parts)


def steps_of(devices):
    flips = [(1, 1), (2, 8), (4, 2), (8, 4)] + [(b, b) for b in (16 << i for i in range(30)) if b < devices]
    return [[(i, i ^ flip[i & 1]) for i in range(devices)] for flip in flips]


def block_order(index):
    core, chip = index & 1, (index >> 1) & 7
    order = []
    for position in range(SPLIT):
        near, here, there, far = (position >> bit & 1 for bit in reversed(range(SCATTERS)))
        owner = core ^ near
        flips = jnp.where(owner == 0, here + there * 2 + far * 4, there + far * 2 + here * 4)
        order.append(owner * 8 + (chip ^ flips))
    return jnp.stack(order).astype(jnp.int32)


def exchanges(keep, send, steps):
    for step in range(SCATTERS):
        got = yield send, steps[step]
        half = keep.shape[0]
        quarter = half // 2 if step < SCATTERS - 1 else 0
        parts = [keep[quarter:] + got[quarter:half]]
        if got.shape[0] > half:
            parts.append(send[half:] + got[half:])
        send = jnp.concatenate(parts, axis=0)
        keep = keep[:quarter] + got[:quarter]
    for step in steps[SCATTERS:]:
        send = send + (yield send, step)
    own, extra = send[:half], send[half:]
    pair = jnp.concatenate([own, (yield own, steps[3])], axis=0)
    four = jnp.concatenate([pair, (yield pair, steps[2])], axis=0)
    other = yield four, steps[1]
    first = yield four, steps[0]
    second = yield other, steps[0]
    return [four, other, first, second], extra


def side_by_side(chains):
    results = [None] * len(chains)
    got = [None] * len(chains)
    while None in results:
        for i, chain in enumerate(chains):
            try:
                send, step = chain.send(got[i])
                got[i] = lax.ppermute(send, BOTH, step)
            except StopIteration as end:
                results[i] = end.value
    return results


def on_device(height, land_sea, patterns):
    days, lon_cells, lat_cells = height.shape
    lat_devices = lax.axis_size("lat")
    lon_devices = lax.axis_size("lon")
    total_rows = lat_cells * lat_devices
    lat_place = lax.axis_index("lat")
    lon_place = lax.axis_index("lon")
    mode_count = patterns.shape[0]
    chunks = [(0, days // 2), (days // 2, days // 2)]
    steps = steps_of(lat_devices * lon_devices)
    up = [(i, i + 1) for i in range(lon_devices - 1)]
    down = [(j, i) for i, j in up]

    first, last = edge_rows(height)
    before = lax.ppermute(last, "lon", up)
    after = lax.ppermute(first, "lon", down)

    rows_index = lat_place * lat_cells + jnp.arange(lat_cells, dtype=jnp.int32)
    coef_east, coef_north = stencil_coefs(rows_index, total_rows)
    ocean = land_sea.astype(F32)
    coefs = jnp.stack([coef_east * ocean, coef_north * ocean])
    place = jnp.stack([lat_place, lon_place]).astype(jnp.int32)
    order = block_order(lon_place * lat_devices + lat_place)
    *totals, energy, near_rows, edge_cols, sent_cols, row_patterns, col_patterns = interior(
        chunks, order, height, coefs, patterns
    )
    pairs = [[(i, i ^ 1) for i in range(lat_devices)]]
    pairs.append([(i, ((i + 1) ^ 1) - 1) for i in range(1, lat_devices - 1)])
    other, paired = (lax.ppermute(sent_cols, "lat", pair) for pair in reversed(pairs))

    chains = []
    for i, chunk in enumerate(chunks):
        last = i == len(chunks) - 1
        keep, send, *more = edge(
            chunk, last, place, totals[i], before, after, near_rows, paired, other, edge_cols,
            coefs, row_patterns, col_patterns, energy,
        )
        chains.append(exchanges(keep, send, steps))
        energy = more[0] if more else energy
    results = side_by_side(chains)
    parts = [part for found, _ in results for part in found]
    energy = results[-1][1][:, :LANES]
    cells_total = 2.0 * days * lon_cells * lon_devices * total_rows
    return covariance(
        cells_total, chunks, mode_count // lat_devices, place, order, energy, parts
    )


def solution(mesh):
    placed = (P(None, "lon", "lat"), P("lon", "lat"), P(None, None, "lon", "lat"))
    return jax.shard_map(
        on_device, mesh=mesh, in_specs=placed, out_specs=P("lon", "lat", None), check_vma=False
    )
```

```python
import functools
import math

import jax
import jax.numpy as jnp
from jax import lax
from jax.experimental import pallas as pl
from jax.experimental.pallas import tpu as pltpu
from jax.sharding import PartitionSpec as P

GRAVITY = 9.81
ROTATION = 7.2921e-05
EARTH_RADIUS = 6371000.0
LAT_SOUTH = 20.0
LAT_SPAN = 45.0
LON_STEP = 1.0 / 12.0

F32 = jnp.float32
BF16 = jnp.bfloat16
BOTH = ("lon", "lat")
LANES = 128
TILE = 8
DAY_BLOCK = 256
SCATTERS = 4
SPLIT = 2**SCATTERS
VMEM = pl.BlockSpec(memory_space=pltpu.VMEM)
SMEM = pl.BlockSpec(memory_space=pltpu.SMEM)
ANY = pl.BlockSpec(memory_space=pl.ANY)
NT = (((1,), (1,)), ((), ()))
NN = (((1,), (0,)), ((), ()))


def like(*shape, dtype=F32):
    return jax.ShapeDtypeStruct(shape, dtype)


def params(mib=24):
    return pltpu.CompilerParams(vmem_limit_bytes=mib << 20)


def stencil_coefs(rows_index, total_rows):
    degrees = LAT_SOUTH + LAT_SPAN * (rows_index.astype(F32) + 0.5) / total_rows
    radians = degrees * (math.pi / 180.0)
    coriolis = 2.0 * ROTATION * jnp.sin(radians)
    north_step = EARTH_RADIUS * (LAT_SPAN / total_rows) * (math.pi / 180.0)
    east_step = EARTH_RADIUS * jnp.cos(radians) * (LON_STEP * math.pi / 180.0)
    return (-GRAVITY / (coriolis * 2.0 * north_step), GRAVITY / (coriolis * 2.0 * east_step))


def edge_rows_kernel(height, first, last, sems):
    copies = [
        pltpu.make_async_copy(height.at[:, row, :], to, sems.at[at])
        for at, (row, to) in enumerate(((0, first), (height.shape[1] - 1, last)))
    ]
    for copy in copies:
        copy.start()
    for copy in copies:
        copy.wait()


def edge_rows(height):
    days, _, lanes = height.shape
    return pl.pallas_call(
        edge_rows_kernel,
        out_shape=[like(days, lanes)] * 2,
        in_specs=[ANY],
        out_specs=[VMEM] * 2,
        scratch_shapes=[pltpu.SemaphoreType.DMA((2,))],
    )(height)


def interior_kernel(chunks, order, height, coefs, patterns_hbm, *refs):
    totals, refs = refs[: len(chunks)], refs[len(chunks) :]
    energy, near_rows, edge_cols, sent_cols, row_patterns, col_patterns, *refs = refs
    patterns, flat, first, second, sem = refs
    cells, lanes = coefs.shape[1:]
    days = height.shape[0] // cells
    modes = patterns.shape[0]
    north_at = cells * lanes
    block = modes // SPLIT
    group_days = lanes // 4
    size = 16 * cells
    step = pl.program_id(0)
    to, source = (lax.broadcasted_iota(jnp.int32, (size, size), dim) for dim in (0, 1))
    swap = ((to // 16 == source % cells) & (to % 16 == source // cells)).astype(BF16)

    copy = pltpu.make_async_copy(patterns_hbm, patterns, sem)

    def lay_out_patterns():
        @pl.loop(0, modes // 16, unroll=8)
        def _(group):
            at = group * 16
            source_row = order[at // block] * block + at % block
            both = jnp.concatenate(
                [
                    patterns[pl.ds(source_row, 16), side].reshape(size, lanes)
                    for side in range(2)
                ],
                axis=1,
            )
            moved = lax.dot_general(swap, both, NN, preferred_element_type=F32).astype(BF16)
            here = pl.ds(pl.multiple_of(at, 16), 16)
            for cell in range(cells):
                rows = slice(cell * 16, cell * 16 + 16)
                flat[here, cell * lanes : (cell + 1) * lanes] = moved[rows, :lanes]
                north = moved[rows, lanes:]
                if cell == 0:
                    row_patterns[here, :lanes] = north
                elif cell == cells - 1:
                    row_patterns[here, lanes:] = north
                else:
                    place = north_at + (cell - 1) * lanes
                    flat[here, place : place + lanes] = north

        width = 2 * cells
        place, column = (lax.broadcasted_iota(jnp.int32, (cells * lanes, width), d) for d in (0, 1))
        wanted = (column % cells) * lanes + (column // cells) * (lanes - 1)
        pick = (place == wanted).astype(BF16)
        col_patterns[...] = lax.dot_general(
            flat[:, :north_at], pick, NN, preferred_element_type=F32
        ).astype(BF16)

    lane = lax.broadcasted_iota(jnp.int32, (TILE, lanes), 1)
    row = lax.broadcasted_iota(jnp.int32, (TILE, lanes), 0)
    inner = (lane > 0) & (lane < lanes - 1)
    east_coefs = [jnp.where(inner, coefs[0, at : at + TILE, :], 0.0) for at in (0, TILE)]
    north_coefs = [coefs[1, 1 : 1 + TILE, :], jnp.where(row < 2, 0.0, coefs[1, 7 : 7 + TILE, :])]

    def some_days(velocity, group, gathered):
        gathered = list(gathered)
        total = jnp.zeros((TILE, lanes), F32)
        easts, norths = [], []
        for day in range(16):
            base = pl.multiple_of((group * 16 + day) * cells, cells)
            halves = [height[pl.ds(base + at, TILE), :] for at in (0, TILE)]
            inside = [height[pl.ds(base + at, TILE), :] for at in (2, 6)]
            diffs = [inside[0] - halves[0], halves[1] - inside[1]]
            for side in range(2):
                plane = halves[side]
                east = pltpu.roll(plane, lanes - 1, 1) - pltpu.roll(plane, 1, 1)
                east = east * east_coefs[side]
                north = diffs[side] * north_coefs[side]
                total = total + east * east + north * north
                easts.append(east)
                norths.append(north)
                place = (group % 2) * 16 + day
                turn = pltpu.roll(plane, 4 * place + 2, 1)
                gathered[side] = jnp.where(lane // 4 == place, turn, gathered[side])
        both = jnp.concatenate(
            [jnp.concatenate(easts).astype(BF16), jnp.concatenate(norths).astype(BF16)], axis=1
        )
        moved = lax.dot_general(swap, both, NN, preferred_element_type=F32).astype(BF16)
        here = pl.ds(pl.multiple_of(group * 16, 16), 16)
        for cell in range(cells):
            rows = slice(cell * 16, cell * 16 + 16)
            velocity[here, cell * lanes : (cell + 1) * lanes] = moved[rows, :lanes]
            if cell < TILE or cell > TILE + 1:
                place = north_at + (cell if cell < TILE else cell - 2) * lanes
                velocity[here, place : place + lanes] = moved[rows, lanes:]
        return gathered, total

    def two_groups(velocity, pair):
        zero = jnp.zeros((TILE, lanes), F32)
        gathered, one = some_days(velocity, pair * 2, [zero, zero])
        gathered, two = some_days(velocity, pair * 2 + 1, gathered)
        energy[...] += one + two
        edge_cols[:, pair * lanes : (pair + 1) * lanes] = jnp.concatenate(gathered)

    def work_out(velocity):
        pairs = days // group_days
        for pair in range(pairs):
            two_groups(velocity, pair)
        middle = (lane % 4 == 1) | (lane % 4 == 2)
        for pair in range(0, pairs, 2):
            for side in range(0, cells, TILE):
                here = edge_cols[side : side + TILE, pair * lanes : (pair + 1) * lanes]
                there = edge_cols[side : side + TILE, (pair + 1) * lanes : (pair + 2) * lanes]
                both = jnp.where(middle, here, pltpu.roll(there, 2, 1))
                sent_cols[side : side + TILE, pair // 2 * lanes : (pair // 2 + 1) * lanes] = both
        for side, cell in enumerate((1, cells - 2)):
            near_rows[side] = height[pl.ds(cell, days, stride=cells), :]

    def project(velocity, to):
        to[...] = lax.dot_general(flat[...], velocity[...], NT, preferred_element_type=F32)

    blocks = (chunks[-1][0] + chunks[-1][1]) // days
    for at in range(blocks + 1):

        @pl.when(step == at)
        def _(at=at):
            now, ago = (first, second) if at % 2 == 0 else (second, first)
            if at == 0:
                copy.start()
                energy[...] = jnp.zeros_like(energy)
            else:
                day = (at - 1) * days
                chunk = max(i for i, (start, _) in enumerate(chunks) if start <= day)
                project(ago, totals[chunk])
            if at < blocks:
                work_out(now)
            if at == 0:
                copy.wait()
                lay_out_patterns()


def interior(chunks, order, height, coefs, patterns):
    days, cells, lanes = height.shape
    modes = patterns.shape[0]
    depth = (2 * cells - 2) * lanes
    day = min(DAY_BLOCK, days)
    blocks = days // day
    now = lambda s: jnp.minimum(s, blocks - 1)

    def totals_spec(start, size):
        index = lambda s: (0, jnp.clip(s - 1 - start // day, 0, size // day - 1))
        return pl.BlockSpec((modes, day), index)

    return pl.pallas_call(
        functools.partial(interior_kernel, chunks),
        grid=(blocks + 1,),
        out_shape=[like(modes, size) for _, size in chunks]
        + [
            like(TILE, lanes),
            like(2, days, lanes),
            like(cells, 4 * days),
            like(cells, 2 * days),
            like(modes, 2 * lanes, dtype=BF16),
            like(modes, 2 * cells, dtype=BF16),
        ],
        in_specs=[
            SMEM,
            pl.BlockSpec((day * cells, lanes), lambda s: (now(s), 0)),
            pl.BlockSpec((2, cells, lanes), lambda s: (0, 0, 0)),
            ANY,
        ],
        out_specs=[totals_spec(*chunk) for chunk in chunks]
        + [
            pl.BlockSpec((TILE, lanes), lambda s: (0, 0)),
            pl.BlockSpec((2, day, lanes), lambda s: (0, now(s), 0)),
            pl.BlockSpec((cells, 4 * day), lambda s: (0, now(s))),
            pl.BlockSpec((cells, 2 * day), lambda s: (0, now(s))),
            pl.BlockSpec((modes, 2 * lanes), lambda s: (0, 0)),
            pl.BlockSpec((modes, 2 * cells), lambda s: (0, 0)),
        ],
        scratch_shapes=[
            pltpu.VMEM(patterns.shape, BF16),
            pltpu.VMEM((modes, depth), BF16),
            pltpu.VMEM((day, depth), BF16),
            pltpu.VMEM((day, depth), BF16),
            pltpu.SemaphoreType.DMA,
        ],
        compiler_params=params(48),
        cost_estimate=pl.CostEstimate(
            flops=2 * modes * depth * days, bytes_accessed=14 << 20, transcendentals=0
        ),
    )(order, height.reshape(days * cells, lanes), coefs, patterns)


def with_edges(chunk, totals, rows, cols, row_patterns, col_patterns):
    days = pl.ds(*chunk)
    added = lax.dot_general(row_patterns[...], rows[days, :], NT, preferred_element_type=F32)
    added = added + lax.dot_general(
        col_patterns[...], cols[:, days], NN, preferred_element_type=F32
    )
    return totals[...] + added


def send_kernel(
    chunks, place, before, after, near_rows, paired, other, edge_cols, coefs, row_patterns,
    col_patterns, energy, *refs,
):
    totals, (rows, cols, *sends) = refs[: len(chunks)], refs[len(chunks) :]
    cells, lanes = coefs.shape[1:]
    days = before.shape[0]
    low = (near_rows[0] - before[...]) * coefs[1, 0:1, :]
    high = (after[...] - near_rows[1]) * coefs[1, cells - 1 : cells, :]
    rows[...] = jnp.concatenate([low.astype(BF16), high.astype(BF16)], axis=1)
    four = lax.broadcasted_iota(jnp.int32, (cells, 4 * days), 1) % 4
    even = place[0] % 2 == 0
    spread = []
    for one, two in ((other, paired), (paired, other)):
        halo = jnp.where(even, one[...], two[...])
        blocks = [halo[:, at : at + lanes] for at in range(0, 2 * days, lanes)]
        spread.append([a for b in blocks for a in (b, pltpu.roll(b, lanes - 2, 1))])
    west, east = (jnp.concatenate(a, axis=1) for a in spread)
    left = (edge_cols[...] - pltpu.roll(west, 2, 1)) * coefs[0, :, 0:1]
    right = (east - pltpu.roll(edge_cols[...], 2, 1)) * coefs[0, :, lanes - 1 : lanes]
    both = jnp.where(four == 3, left, jnp.where(four == 2, right, 0.0))
    packed = both.astype(BF16)
    wide = 4 * lanes
    packed = jnp.concatenate([packed[:, at : at + wide] for at in range(0, 4 * days, wide)], axis=0)
    place, column = (lax.broadcasted_iota(jnp.int32, (wide, 2 * lanes), d) for d in (0, 1))
    pick = (place == 4 * (column % lanes) + 3 - column // lanes).astype(BF16)
    sides = lax.dot_general(packed, pick, NN, preferred_element_type=F32).astype(BF16)
    cols[...] = jnp.concatenate(
        [
            jnp.concatenate([sides[at : at + cells, :lanes], sides[at : at + cells, lanes:]], axis=0)
            for at in range(0, sides.shape[0], cells)
        ],
        axis=1,
    )
    half = totals[0].shape[0]
    for chunk, total, send in zip(chunks, totals, sends):
        send[:half, :] = with_edges(chunk, total, rows, cols, row_patterns, col_patterns)
    squares = energy[...] + (low * low + high * high).reshape(-1, TILE, lanes).sum(axis=0)
    across = both * both
    for at in range(0, 4 * days, lanes):
        squares = squares + across[:, at : at + lanes].reshape(-1, TILE, lanes).sum(axis=0)
    sends[-1][half:, :] = jnp.zeros((TILE, sends[-1].shape[1]), F32)
    sends[-1][half:, :lanes] = squares


def keep_kernel(chunks, rows, cols, row_patterns, col_patterns, *refs):
    totals, keeps = refs[: len(chunks)], refs[len(chunks) :]
    for chunk, total, keep in zip(chunks, totals, keeps):
        keep[...] = with_edges(chunk, total, rows, cols, row_patterns, col_patterns)


def half_specs(arrays, part):
    return [pl.BlockSpec((a.shape[0] // 2, a.shape[1]), lambda s: (part, 0)) for a in arrays]


def edge(chunks, place, totals, before, after, near_rows, paired, other, edge_cols, coefs,
         row_patterns, col_patterns, energy):
    half = totals[0].shape[0] // 2
    cells, lanes = coefs.shape[1:]
    days = before.shape[0]
    whole = lambda a: pl.BlockSpec(a.shape, lambda s: (0,) * a.ndim)
    outs = [like(days, 2 * lanes, dtype=BF16), like(2 * cells, days, dtype=BF16)]
    outs += [like(half + TILE * (i == len(chunks) - 1), size) for i, (_, size) in enumerate(chunks)]
    wholes = (before, after, near_rows, paired, other, edge_cols, coefs)
    patterns = (row_patterns, col_patterns)
    rows, cols, *sends = pl.pallas_call(
        functools.partial(send_kernel, chunks),
        grid=(1,),
        out_shape=outs,
        in_specs=[SMEM]
        + [whole(a) for a in wholes]
        + half_specs(patterns, 1)
        + [whole(energy)]
        + half_specs(totals, 1),
        out_specs=[whole(a) for a in outs],
        compiler_params=params(),
    )(place, *wholes, *patterns, energy, *totals)
    keeps = [like(half, size) for _, size in chunks]
    keeps = pl.pallas_call(
        functools.partial(keep_kernel, chunks),
        grid=(1,),
        out_shape=keeps,
        in_specs=[whole(rows), whole(cols)] + half_specs(patterns, 0) + half_specs(totals, 0),
        out_specs=[whole(a) for a in keeps],
        compiler_params=params(),
    )(rows, cols, *patterns, *totals)
    return keeps, sends


def covariance_kernel(cells_total, chunks, place, order, energy, *refs):
    parts, (out, full, high, low) = refs[:-4], refs[-4:]
    modes, days = full.shape
    block = modes // SPLIT
    per_chunk = len(parts) // len(chunks)
    for at, (start, size) in enumerate(chunks):
        position = 0
        for part in parts[at * per_chunk : (at + 1) * per_chunk]:
            for piece in range(part.shape[0] // block):
                to = pl.ds(pl.multiple_of(order[position] * block, block), block)
                full[to, start : start + size] = part[piece * block : (piece + 1) * block, :]
                position += 1
    centered = full[...] - jnp.sum(full[...], axis=1, keepdims=True) * (1.0 / days)
    full[...] = centered
    upper = centered.astype(BF16)
    high[...] = upper
    low[...] = (centered - upper.astype(F32)).astype(BF16)
    rows = out.shape[1]
    lag = place[1]
    mine = full[pl.ds(pl.multiple_of(place[0] * rows, rows), rows), :]
    mine = pltpu.roll(mine, days - lag, 1)
    day = lax.broadcasted_iota(jnp.int32, mine.shape, 1)
    mine = jnp.where(day < days - lag, mine, 0.0)
    mine_high = mine.astype(BF16)
    mine_low = (mine - mine_high.astype(F32)).astype(BF16)
    dot = lambda a, b: lax.dot_general(a, b, NT, preferred_element_type=F32)
    product = dot(mine_low, high[...]) + dot(mine_high, low[...]) + dot(mine_high, high[...])
    total = jnp.sum(energy[...], axis=(0, 1), keepdims=True)
    spread = total / cells_total + 1e-06
    out[0] = product / (spread * (days - lag).astype(F32))


def covariance(cells_total, chunks, rows, place, order, energy, parts):
    modes = 4 * parts[0].shape[0]
    days = sum(size for _, size in chunks)
    return pl.pallas_call(
        functools.partial(covariance_kernel, cells_total, chunks),
        out_shape=like(1, rows, modes),
        in_specs=[SMEM, SMEM] + [VMEM] * (1 + len(parts)),
        out_specs=VMEM,
        scratch_shapes=[
            pltpu.VMEM((modes, days), F32),
            pltpu.VMEM((modes, days), BF16),
            pltpu.VMEM((modes, days), BF16),
        ],
        compiler_params=params(),
    )(place, order, energy, *parts)


def steps_of(devices):
    flips = [(1, 1), (2, 8), (4, 2), (8, 4)] + [(b, b) for b in (16 << i for i in range(30)) if b < devices]
    return [[(i, i ^ flip[i & 1]) for i in range(devices)] for flip in flips]


def block_order(index):
    core, chip = index & 1, (index >> 1) & 7
    order = []
    for position in range(SPLIT):
        near, here, there, far = (position >> bit & 1 for bit in reversed(range(SCATTERS)))
        owner = core ^ near
        flips = jnp.where(owner == 0, here + there * 2 + far * 4, there + far * 2 + here * 4)
        order.append(owner * 8 + (chip ^ flips))
    return jnp.stack(order).astype(jnp.int32)


def exchanges(keep, send, steps):
    for step in range(SCATTERS):
        got = yield send, steps[step]
        half = keep.shape[0]
        quarter = half // 2 if step < SCATTERS - 1 else 0
        parts = [keep[quarter:] + got[quarter:half]]
        if got.shape[0] > half:
            parts.append(send[half:] + got[half:])
        send = jnp.concatenate(parts, axis=0)
        keep = keep[:quarter] + got[:quarter]
    for step in steps[SCATTERS:]:
        send = send + (yield send, step)
    own, extra = send[:half], send[half:]
    pair = jnp.concatenate([own, (yield own, steps[3])], axis=0)
    four = jnp.concatenate([pair, (yield pair, steps[2])], axis=0)
    other = yield four, steps[1]
    first = yield four, steps[0]
    second = yield other, steps[0]
    return [four, other, first, second], extra


def side_by_side(chains):
    results = [None] * len(chains)
    got = [None] * len(chains)
    while None in results:
        for i, chain in enumerate(chains):
            try:
                send, step = chain.send(got[i])
                got[i] = lax.ppermute(send, BOTH, step)
            except StopIteration as end:
                results[i] = end.value
    return results


def on_device(height, land_sea, patterns):
    days, lon_cells, lat_cells = height.shape
    lat_devices = lax.axis_size("lat")
    lon_devices = lax.axis_size("lon")
    total_rows = lat_cells * lat_devices
    lat_place = lax.axis_index("lat")
    lon_place = lax.axis_index("lon")
    mode_count = patterns.shape[0]
    chunks = [(0, days // 2), (days // 2, days // 2)]
    steps = steps_of(lat_devices * lon_devices)
    up = [(i, i + 1) for i in range(lon_devices - 1)]
    down = [(j, i) for i, j in up]

    first, last = edge_rows(height)
    before = lax.ppermute(last, "lon", up)
    after = lax.ppermute(first, "lon", down)

    rows_index = lat_place * lat_cells + jnp.arange(lat_cells, dtype=jnp.int32)
    coef_east, coef_north = stencil_coefs(rows_index, total_rows)
    ocean = land_sea.astype(F32)
    coefs = jnp.stack([coef_east * ocean, coef_north * ocean])
    place = jnp.stack([lat_place, lon_place]).astype(jnp.int32)
    order = block_order(lon_place * lat_devices + lat_place)
    *totals, energy, near_rows, edge_cols, sent_cols, row_patterns, col_patterns = interior(
        chunks, order, height, coefs, patterns
    )
    pairs = [[(i, i ^ 1) for i in range(lat_devices)]]
    pairs.append([(i, ((i + 1) ^ 1) - 1) for i in range(1, lat_devices - 1)])
    paired, other = (lax.ppermute(sent_cols, "lat", pair) for pair in pairs)

    keeps, sends = edge(
        chunks, place, totals, before, after, near_rows, paired, other, edge_cols, coefs,
        row_patterns, col_patterns, energy,
    )
    chains = [exchanges(keep, send, steps) for keep, send in zip(keeps, sends)]
    results = side_by_side(chains)
    parts = [part for found, _ in results for part in found]
    energy = results[-1][1][:, :LANES]
    cells_total = 2.0 * days * lon_cells * lon_devices * total_rows
    return covariance(
        cells_total, chunks, mode_count // lat_devices, place, order, energy, parts
    )


def solution(mesh):
    placed = (P(None, "lon", "lat"), P("lon", "lat"), P(None, None, "lon", "lat"))
    return jax.shard_map(
        on_device, mesh=mesh, in_specs=placed, out_specs=P("lon", "lat", None), check_vma=False
    )
```
